256 devices in a mesh: aux: 8 (over x_hi, y), blk: 32 (over z, x_lo, core).
Axes of the slice: x: 4 (x_hi: 2, x_lo: 2; x = x_hi * 2 + x_lo), y: 4, z: 8, core: 2. Of those that a mesh axis runs over, the one named last changes fastest.
Arguments:
- three_center: bfloat16 [3072, 8, 128, 128], P(('aux', 'blk')), may hold values from -6 to 6
- slot_block: int32 [3072], P(('aux', 'blk')), may hold values from 0 to 47
- slot_aux: int32 [3072], P(('aux', 'blk')), may hold values from 0 to 1
- live_slots: int32 [256], P(('aux', 'blk')), may hold values from 1 to 12, as said below
- vir_coef: bfloat16 [6144, 256], replicated, may hold values from -0.00169145587 to 0.00169145587
- eps_occ: float32 [4000], replicated, may hold values from -1.5 to -0.3
- eps_vir: float32 [256], replicated, may hold values from 0.2 to 3
- occ_index: int32 [8], replicated, may hold values from 0 to 3999, as said below
Outputs:
- amplitudes: float32 [8, 256, 8, 256], P('aux', 'blk')
- pair_energy: float32 [8, 8], P('aux')
The draws below stay inside these ranges and needn't reach their ends.
Inputs may be any that keep to these rules, and one draw needn't show every extreme that they name: The slots in use on a device are its first live_slots ones; the others hold data that is not used. Some device holds exactly 12 slots in use in every draw. `occ_index`: the indices are distinct; the first and the last occupied orbital of the system are in every batch.
All inputs are finite; a program needn't handle non-finite values.
Results may differ from the reference program's by a relative error of at most 0.0035.
Values may be sent and summed in bfloat16 or wider, within the bound.
No kernel may reach another device: no remote copies, remote signals or barrier semaphores. Data moves between devices by JAX's collectives and lax.ppermute only.
A program may use at most 64 MiB of HBM per device.

```python
import jax
import jax.numpy as jnp
from jax import lax

VIRTUAL = 256
AO_BLOCK = 128
AUX_BLOCK = 128
AUX_BLOCKS_DEV = 2
SLOT_DEV = 12
AO_BLOCKS = 48
OCC_ALL = 4000
DEVICE_COUNT = 256
OCC_BATCH = 8
AUX_TOTAL = 65536
SLOT_ALL = 3072


def sample_values(key, shape, limit):
    return jnp.clip(jax.random.normal(key, shape, jnp.float32), -limit, limit)


def draw_three_center(key, part):
    offsets = jax.random.randint(jax.random.fold_in(key, 3), (OCC_BATCH,), 1, AO_BLOCK)
    places = (jnp.arange(AO_BLOCK)[None, :] + offsets[:, None]) % AO_BLOCK
    pair_weight = 0.35 ** 0.5
    own_weight = 0.3 ** 0.5
    key_shared = jax.random.fold_in(key, 41)
    key_own = jax.random.fold_in(key, 43)

    def one_slot(slot_id):
        shared = sample_values(jax.random.fold_in(key_shared, slot_id), (AUX_BLOCK, AO_BLOCK), 3.45)
        own_part = sample_values(jax.random.fold_in(key_own, slot_id), (OCC_BATCH, AUX_BLOCK, AO_BLOCK), 3.45)
        rolled = jnp.transpose(jnp.take(shared, places, axis=1), (1, 0, 2))
        mixed = pair_weight * (shared[None] + rolled) + own_weight * own_part
        return mixed.astype(jnp.bfloat16)
    return lax.map(one_slot, jnp.arange(SLOT_ALL))


def draw_vir_coef(key, part):
    scale_factor = (AO_BLOCK * AUX_TOTAL * 1.5) ** (-0.5)
    common_weight = 0.35 ** 0.5
    own_weight = 0.65 ** 0.5
    common = sample_values(jax.random.fold_in(key, 51), (AO_BLOCK, VIRTUAL), 4.29)
    own_part = sample_values(jax.random.fold_in(key, 53), (AO_BLOCKS * AO_BLOCK, VIRTUAL), 4.29)
    values = scale_factor * (common_weight * jnp.tile(common, (AO_BLOCKS, 1)) + own_weight * own_part)
    return values.astype(jnp.bfloat16)


def draw_live_slots(key, part):
    key_base = jax.random.fold_in(key, 11)
    key_busy = jax.random.fold_in(key, 23)
    key_chosen = jax.random.fold_in(key, 37)
    base = jax.random.randint(key_base, (DEVICE_COUNT,), 1, SLOT_DEV // 2 + 1)
    busy = jax.random.randint(key_busy, (DEVICE_COUNT,), 0, 8) == 0
    chosen = jax.random.randint(key_chosen, (), 0, DEVICE_COUNT)
    filled = jnp.logical_or(busy, jnp.arange(DEVICE_COUNT) == chosen)
    return jnp.where(filled, SLOT_DEV, base).astype(jnp.int32)


def draw_occ_index(key, part):
    middle = jax.random.permutation(jax.random.fold_in(key, 5), OCC_ALL - 2)[:OCC_BATCH - 2] + 1
    ends = jnp.array([0, OCC_ALL - 1], dtype=jnp.int32)
    values = jnp.concatenate([ends, middle.astype(jnp.int32)])
    order = jax.random.permutation(jax.random.fold_in(key, 7), OCC_BATCH)
    return jnp.take(values, order).astype(jnp.int32)


def place_ends(values, rng, least, largest):
    shape = values.shape
    place = [jax.random.randint(jax.random.fold_in(rng, axis), (), 0, shape[axis]) for axis in range(len(shape))]
    values = values.at[tuple(place)].set(least)
    longest = shape.index(max(shape))
    place[longest] = (place[longest] + 1) % shape[longest]
    return values.at[tuple(place)].set(largest)


def setup_inputs(seed: int = 0) -> dict:
    arg_keys = jax.random.split(jax.random.key(seed), 9)
    three_center = draw_three_center(jax.random.fold_in(arg_keys[8], 71), 0)
    slot_block = place_ends(jax.random.randint(arg_keys[1], (SLOT_ALL,), 0, AO_BLOCKS), jax.random.fold_in(arg_keys[1], 1), 0, AO_BLOCKS - 1).astype(jnp.int32)
    slot_aux = place_ends(jax.random.randint(arg_keys[2], (SLOT_ALL,), 0, AUX_BLOCKS_DEV), jax.random.fold_in(arg_keys[2], 1), 0, AUX_BLOCKS_DEV - 1).astype(jnp.int32)
    live_slots = draw_live_slots(jax.random.fold_in(arg_keys[8], 71), 0)
    vir_coef = draw_vir_coef(jax.random.fold_in(arg_keys[8], 71), 0)
    eps_occ = jnp.clip(jax.random.uniform(arg_keys[5], (OCC_ALL,), jnp.float32, -1.5, -0.3), -1.5, -0.3)
    eps_vir = jnp.clip(jax.random.uniform(arg_keys[6], (VIRTUAL,), jnp.float32, 0.2, 3.0), 0.2, 3.0)
    occ_index = draw_occ_index(jax.random.fold_in(arg_keys[8], 71), 0)
    return dict(three_center=three_center, slot_block=slot_block, slot_aux=slot_aux, live_slots=live_slots, vir_coef=vir_coef, eps_occ=eps_occ, eps_vir=eps_vir, occ_index=occ_index)


def reference(three_center, slot_block, slot_aux, live_slots, vir_coef, eps_occ, eps_vir, occ_index):
    coef_blocks = vir_coef.reshape(AO_BLOCKS, AO_BLOCK, VIRTUAL)

    def transform(inputs):
        blocks, block_ids, aux_ids, live_count = inputs
        coefficients = jnp.take(coef_blocks, block_ids, axis=0).astype(jnp.float32)
        products = jnp.einsum('soqn,snv->soqv', blocks.astype(jnp.float32), coefficients)
        keep = (jnp.arange(SLOT_DEV) < live_count).astype(jnp.float32)
        select = (aux_ids[:, None] == jnp.arange(AUX_BLOCKS_DEV)[None, :]).astype(jnp.float32)
        select = select * keep[:, None]
        return jnp.einsum('sk,soqv->kqov', select, products).astype(jnp.bfloat16)

    per_device = lax.map(transform, (
        three_center.reshape(DEVICE_COUNT, SLOT_DEV, OCC_BATCH, AUX_BLOCK, AO_BLOCK),
        slot_block.reshape(DEVICE_COUNT, SLOT_DEV),
        slot_aux.reshape(DEVICE_COUNT, SLOT_DEV),
        live_slots))
    half_ints = per_device.reshape(AUX_TOTAL, OCC_BATCH * VIRTUAL).astype(jnp.float32)
    coulomb = jnp.dot(half_ints.T, half_ints, preferred_element_type=jnp.float32)
    coulomb = coulomb.reshape(OCC_BATCH, VIRTUAL, OCC_BATCH, VIRTUAL)
    occ_levels = jnp.take(eps_occ, occ_index)
    denominator = (occ_levels[:, None, None, None] + occ_levels[None, None, :, None]
                   - eps_vir[None, :, None, None] - eps_vir[None, None, None, :])
    amplitudes = coulomb / denominator
    crossed = jnp.transpose(coulomb, (0, 3, 2, 1))
    pair_energy = jnp.sum(coulomb * (2.0 * coulomb - crossed) / denominator, axis=(1, 3))
    return amplitudes, pair_energy
```

```python
import functools

import jax
import jax.numpy as jnp
from jax import lax
from jax.experimental import pallas as pl
from jax.experimental.pallas import tpu as pltpu
from jax.sharding import Mesh
from jax.sharding import PartitionSpec as P

F32 = jnp.float32
BF16 = jnp.bfloat16
OCC = 8
VIR = 256
SPAN = 128
SLOTS = 12
KINDS = 2
ROWS = 256
AUX = ("xh", "y")
BLK = ("z", "xl", "core")
X = ("xh", "xl")

VMEM = pl.BlockSpec(memory_space=pltpu.VMEM)
SMEM = pl.BlockSpec(memory_space=pltpu.SMEM)
ANYWHERE = pl.BlockSpec(memory_space=pl.ANY)


def params(mib):
    return pltpu.CompilerParams(vmem_limit_bytes=mib * 2**20)


def half_kernel(block_ref, kind_ref, live_ref, three_ref, coef_ref, out_ref, three, coef, weights, sems):
    copies = []
    for s in range(SLOTS):
        first = pl.multiple_of(block_ref[s] * SPAN, SPAN)
        copies.append(pltpu.make_async_copy(coef_ref.at[pl.ds(first, SPAN)], coef.at[s], sems.at[s]))
    for s in range(SLOTS):
        copies.append(
            pltpu.make_async_copy(three_ref.at[s], three.at[:, :, pl.ds(s * SPAN, SPAN)], sems.at[SLOTS + s])
        )
    for copy in copies:
        copy.start()
    for s in range(SLOTS):
        copies[s].wait()
        values = coef[s]
        for k in range(KINDS):
            used = jnp.logical_and(kind_ref[s] == k, s < live_ref[0])
            weights[pl.ds(s * SPAN, SPAN), pl.ds(k * VIR, VIR)] = jnp.where(used, values, jnp.zeros_like(values))
    for s in range(SLOTS):
        copies[SLOTS + s].wait()
    for o in range(0, OCC, 4):
        left = three[pl.ds(o, 4)].reshape(4 * SPAN, SLOTS * SPAN)
        done = jnp.dot(left, weights[...], preferred_element_type=F32).astype(BF16)
        for i in range(4):
            for k in range(KINDS):
                out_ref[o + i, pl.ds(k * SPAN, SPAN), :] = done[i * SPAN : (i + 1) * SPAN, k * VIR : (k + 1) * VIR]


def half_transform(slot_block, slot_aux, live_slots, three_center, vir_coef):
    return pl.pallas_call(
        half_kernel,
        out_shape=jax.ShapeDtypeStruct((OCC, ROWS, VIR), BF16),
        in_specs=[SMEM, SMEM, SMEM, ANYWHERE, ANYWHERE],
        out_specs=VMEM,
        scratch_shapes=[
            pltpu.VMEM((OCC, SPAN, SLOTS * SPAN), BF16),
            pltpu.VMEM((SLOTS, SPAN, VIR), BF16),
            pltpu.VMEM((SLOTS * SPAN, KINDS * VIR), BF16),
            pltpu.SemaphoreType.DMA((2 * SLOTS,)),
        ],
        compiler_params=params(24),
    )(slot_block, slot_aux, live_slots, three_center, vir_coef)


def partial_kernel(place_ref, own_ref, other_ref, *rest):
    outs, left = rest[:10], rest[10]
    x, y, core = place_ref[0], place_ref[1], place_ref[2]
    row = lax.broadcasted_iota(jnp.int32, (128, VIR), 0)
    col = lax.broadcasted_iota(jnp.int32, (128, VIR), 1)
    low, z, r = row // 64, (row // 8) % 8, row % 8
    pick = (col == z * 32 + low * 16 + core * 8 + r).astype(F32).astype(BF16)

    def turned(ref, o, rows):
        return lax.dot_general(rows, ref[o], (((1,), (1,)), ((), ())), preferred_element_type=F32).astype(BF16)

    def send(axis, first_j):
        ahead, back, one, minus, own = outs[axis * 5 : axis * 5 + 5]
        places = {
            (2, 0): (ahead, 0), (1, 1): (ahead, 1), (2, 1): (back, 0), (3, 0): (back, 1),
            (1, 0): (one, None), (3, 1): (minus, None), (0, 0): (own, 0), (0, 1): (own, 1),
        }
        for j in range(4):
            right = jnp.concatenate([own_ref[first_j + j], other_ref[first_j + j]], axis=0)
            done = jnp.dot(left[...], right, preferred_element_type=F32).astype(BF16)
            for d in range(4):
                for h in range(2):
                    ref, which = places[d, h]
                    for u in range(2):
                        at = (d * 4 + h * 2 + u) * 64
                        part = done[at : at + 64]
                        if which is None:
                            ref[u, j] = part
                        else:
                            ref[which, u, j] = part

    for d in range(4):
        for h in range(2):
            o = h * 4 + lax.rem(y + d, 4)
            rows = pl.ds((d * 2 + h) * 128, 128)
            left[rows, pl.ds(0, ROWS)] = turned(own_ref, o, pick)
            left[rows, pl.ds(ROWS, ROWS)] = turned(other_ref, o, pick)
    send(0, 0)
    row = lax.broadcasted_iota(jnp.int32, (64, VIR), 0)
    col = lax.broadcasted_iota(jnp.int32, (64, VIR), 1)
    for d in range(4):
        to = lax.rem(x + d, 4)
        pick = (col == row // 8 * 32 + lax.rem(to, 2) * 16 + core * 8 + row % 8).astype(F32).astype(BF16)
        for h in range(4):
            o = to // 2 * 4 + h
            rows = pl.ds((d * 4 + h) * 64, 64)
            left[rows, pl.ds(0, ROWS)] = turned(own_ref, o, pick)
            left[rows, pl.ds(ROWS, ROWS)] = turned(other_ref, o, pick)
    send(1, 4)


def partial(place, own, other):
    pair = jax.ShapeDtypeStruct((2, 2, 4, 64, VIR), BF16)
    single = jax.ShapeDtypeStruct((2, 4, 64, VIR), BF16)
    return pl.pallas_call(
        partial_kernel,
        out_shape=[pair, pair, single, single, pair] * 2,
        in_specs=[SMEM, VMEM, VMEM],
        out_specs=[VMEM] * 10,
        scratch_shapes=[pltpu.VMEM((1024, 2 * ROWS), BF16)],
        compiler_params=params(40),
    )(place, own, other)


def first_sum_kernel(place_ref, *refs):
    ins, outs, kept = refs[:10], refs[10:18], refs[18]
    for axis in range(2):
        own, from_back, from_ahead, last_back, last_ahead = ins[axis * 5 : axis * 5 + 5]
        at = place_ref[axis]
        for h, (one, two) in enumerate(((from_ahead, last_back), (from_back, last_ahead))):
            for u in range(2):
                for j in range(4):
                    total = own[h, u, j].astype(F32) + one[1, u, j].astype(F32) + two[u, j].astype(F32)
                    kept[h * 2 + u, j] = total.astype(BF16)
        for d in range(4):
            outs[axis * 4 + d][...] = kept[lax.rem(at + d, 4)]


def first_sum(place, ins):
    out = jax.ShapeDtypeStruct((4, 64, VIR), BF16)
    return pl.pallas_call(
        first_sum_kernel,
        out_shape=[out] * 8,
        in_specs=[SMEM] + [VMEM] * 10,
        out_specs=[VMEM] * 8,
        scratch_shapes=[pltpu.VMEM((4, 4, 64, VIR), BF16)],
        compiler_params=params(24),
    )(place, *ins)


def second_sum_kernel(*refs):
    ins, out = refs[:8], refs[8]
    for half in range(2):
        for j in range(4):
            total = ins[half * 4][j].astype(F32)
            for d in range(1, 4):
                total = total + ins[half * 4 + d][j].astype(F32)
            for z in range(8):
                out[z, half * 4 + j] = total[z * 8 : z * 8 + 8]


def second_sum(ins):
    return pl.pallas_call(
        second_sum_kernel,
        out_shape=jax.ShapeDtypeStruct((8, OCC, 8, VIR), F32),
        in_specs=[VMEM] * 8,
        out_specs=VMEM,
        compiler_params=params(24),
    )(*ins)


def finish_kernel(parts_ref, below_ref, direct_ref, cross_ref, amp_ref):
    total = parts_ref[0]
    for z in range(1, 8):
        total = total + parts_ref[z]
    direct_ref[...] = total
    cross_ref[...] = total.astype(BF16)
    amp = total / below_ref[...]
    for j in range(OCC):
        for r in range(8):
            amp_ref[r, pl.ds(j, 1), :] = amp[j, r : r + 1, :]


def finish(parts, below):
    full = (OCC, 8, VIR)
    return pl.pallas_call(
        finish_kernel,
        out_shape=[jax.ShapeDtypeStruct(full, F32), jax.ShapeDtypeStruct(full, BF16), jax.ShapeDtypeStruct((8, OCC, VIR), F32)],
        in_specs=[VMEM] * 2,
        out_specs=[VMEM] * 3,
        compiler_params=params(16),
    )(parts, below)


def energy_kernel(direct_ref, cross_ref, below_ref, out_ref):
    direct = direct_ref[...]
    terms = direct * (2.0 * direct - cross_ref[...].astype(F32)) / below_ref[...]
    out_ref[...] = jnp.broadcast_to(jnp.sum(terms, axis=(1, 2), keepdims=True)[:, 0], (OCC, 128))


def energy(direct, cross, below):
    return pl.pallas_call(
        energy_kernel,
        out_shape=jax.ShapeDtypeStruct((OCC, 128), F32),
        in_specs=[VMEM] * 3,
        out_specs=VMEM,
        compiler_params=params(16),
    )(direct, cross, below)


def moved(x, axis, by):
    n = lax.axis_size(axis)
    return lax.ppermute(x, axis, [(i, (i + by) % n) for i in range(n)])


def body(three_center, slot_block, slot_aux, live_slots, vir_coef, eps_occ, eps_vir, occ_index):
    x, y, core = lax.axis_index(X), lax.axis_index("y"), lax.axis_index("core")
    place = jnp.stack([x, y, core]).astype(jnp.int32)
    own = half_transform(slot_block, slot_aux, live_slots, three_center, vir_coef)
    other = moved(own, "core", 1)
    parts = partial(place, own, other)
    got = []
    for axis, (ahead, back, one, minus, mine) in zip(("y", X), (parts[:5], parts[5:])):
        got.append((axis, moved(ahead, axis, 1), moved(back, axis, -1), one, minus, mine))
    ins = []
    for axis, from_back, from_ahead, one, minus, mine in got:
        one = (one.astype(F32) + from_back[0].astype(F32)).astype(BF16)
        minus = (minus.astype(F32) + from_ahead[0].astype(F32)).astype(BF16)
        ins += [mine, from_back, from_ahead, moved(one, axis, 1), moved(minus, axis, -1)]
    parts = first_sum(place, ins)
    ins = []
    for axis, group in zip((X, "y"), (parts[:4], parts[4:])):
        ins += [group[0]] + [moved(group[d], axis, d) for d in range(1, 4)]
    parts = lax.all_to_all(second_sum(ins), "z", 0, 0, tiled=True)

    occ_row, first_vir = lax.axis_index(AUX), lax.axis_index(BLK) * 8
    levels = jnp.take(eps_occ, occ_index)
    own_level = jnp.sum(jnp.where(jnp.arange(OCC) == occ_row, levels, 0.0))
    vir_levels = lax.dynamic_slice_in_dim(eps_vir, first_vir, 8, 0)
    below = own_level + levels[:, None, None] - vir_levels[None, :, None] - eps_vir[None, None, :]

    direct, cross, amplitudes = finish(parts, below)
    cross = lax.all_to_all(cross, AUX, 0, 0, tiled=True)
    pair = energy(direct, cross, below)
    copies = jnp.broadcast_to(pair, (32, OCC, 128))
    pair = jnp.sum(lax.all_to_all(copies, BLK, 0, 0, tiled=True), axis=0)[:, 0]
    return amplitudes[None], pair[None]


def solution(mesh):
    fine = Mesh(mesh.devices.reshape(2, 4, 8, 2, 2), ("xh", "y", "z", "xl", "core"))
    every = AUX + BLK
    in_specs = (P(every, None, None, None), P(every), P(every), P(every), P(), P(), P(), P())
    out_specs = (P(AUX, BLK, None, None), P(AUX, None))
    return jax.shard_map(body, mesh=fine, in_specs=in_specs, out_specs=out_specs, check_vma=False)
```

```python
import jax
import jax.numpy as jnp
from jax import lax
from jax.experimental import pallas as pl
from jax.experimental.pallas import tpu as pltpu
from jax.sharding import Mesh
from jax.sharding import PartitionSpec as P

F32 = jnp.float32
BF16 = jnp.bfloat16
OCC = 8
VIR = 256
SPAN = 128
SLOTS = 12
KINDS = 2
ROWS = 256
AUX = ("xh", "y")
BLK = ("z", "xl", "core")
X = ("xh", "xl")

VMEM = pl.BlockSpec(memory_space=pltpu.VMEM)
SMEM = pl.BlockSpec(memory_space=pltpu.SMEM)
HBM = pl.BlockSpec(memory_space=pltpu.HBM)


def params(mib):
    return pltpu.CompilerParams(vmem_limit_bytes=mib * 2**20)


def half_kernel(block_hbm, kind_hbm, live_hbm, three_ref, coef_ref, out_ref, block_ref, kind_ref, live_ref, three, coef, weights, sems):
    small = [
        pltpu.make_async_copy(here, there, sems.at[3 * SLOTS + i])
        for i, (here, there) in enumerate(((block_hbm, block_ref), (kind_hbm, kind_ref), (live_hbm, live_ref)))
    ]
    for copy in small:
        copy.start()
    large = []
    for half in range(2):
        for s in range(SLOTS):
            rows, columns = pl.ds(half * 4, 4), pl.ds(s * SPAN, SPAN)
            large.append(
                pltpu.make_async_copy(three_ref.at[s, rows], three.at[rows, :, columns], sems.at[(1 + half) * SLOTS + s])
            )
    for copy in large[:SLOTS]:
        copy.start()
    for copy in small:
        copy.wait()
    copies = []
    for s in range(SLOTS):
        first = pl.multiple_of(block_ref[s] * SPAN, SPAN)
        copies.append(pltpu.make_async_copy(coef_ref.at[pl.ds(first, SPAN)], coef.at[s], sems.at[s]))
        copies[s].start()
    for copy in large[SLOTS:]:
        copy.start()
    for s in range(SLOTS):
        copies[s].wait()
        values = coef[s]
        for k in range(KINDS):
            used = jnp.logical_and(kind_ref[s] == k, s < live_ref[0])
            weights[pl.ds(s * SPAN, SPAN), pl.ds(k * VIR, VIR)] = jnp.where(used, values, jnp.zeros_like(values))
    for half in range(2):
        for s in range(SLOTS):
            large[half * SLOTS + s].wait()
        left = three[pl.ds(half * 4, 4)].reshape(4 * SPAN, SLOTS * SPAN)
        done = jnp.dot(left, weights[...], preferred_element_type=F32).astype(BF16)
        for i in range(4):
            for k in range(KINDS):
                out_ref[half * 4 + i, pl.ds(k * SPAN, SPAN), :] = done[i * SPAN : (i + 1) * SPAN, k * VIR : (k + 1) * VIR]


def half_transform(slot_block, slot_aux, live_slots, three_center, vir_coef):
    return pl.pallas_call(
        half_kernel,
        out_shape=jax.ShapeDtypeStruct((OCC, ROWS, VIR), BF16),
        in_specs=[HBM] * 5,
        out_specs=VMEM,
        scratch_shapes=[
            pltpu.SMEM((SLOTS,), jnp.int32),
            pltpu.SMEM((SLOTS,), jnp.int32),
            pltpu.SMEM((1,), jnp.int32),
            pltpu.VMEM((OCC, SPAN, SLOTS * SPAN), BF16),
            pltpu.VMEM((SLOTS, SPAN, VIR), BF16),
            pltpu.VMEM((SLOTS * SPAN, KINDS * VIR), BF16),
            pltpu.SemaphoreType.DMA((3 * SLOTS + 3,)),
        ],
        compiler_params=params(24),
    )(slot_block, slot_aux, live_slots, three_center, vir_coef)


PLACES = {
    (2, 0): (0, 0), (1, 1): (0, 1), (2, 1): (1, 0), (3, 0): (1, 1),
    (1, 0): (2, None), (3, 1): (3, None), (0, 0): (4, 0), (0, 1): (4, 1),
}


def product(core, first_j, turned, own_ref, other_ref, done):
    for half in range(2):
        columns = pl.ds(pl.multiple_of(lax.rem(core + half, 2) * 128, 128), 128)
        for pair in range(2):
            j = first_j + 2 * pair
            right = jnp.concatenate(
                [jnp.concatenate([ref[j + i, :, columns] for ref in (own_ref, other_ref)], axis=0) for i in range(2)],
                axis=1,
            )
            whole = jnp.dot(turned[half], right, preferred_element_type=F32).astype(BF16)
            done[half, pair] = whole.reshape(OCC, 128, 256)


def tile(done, half, j, o, low):
    lane = lax.broadcasted_iota(jnp.int32, (64, 128), 1)
    columns = pl.ds(j % 2 * 128, 128)
    first, second = done[half, j // 2, o, 0:64, columns], done[half, j // 2, o, 64:128, columns]
    return jnp.where(lax.rem(lane // 64 + low, 2) == 0, first.astype(F32), second.astype(F32)).astype(BF16)


def along_y_kernel(place_ref, own_ref, other_ref, *rest):
    outs, turned, done = rest[:5], rest[5], rest[6]
    y, core = place_ref[1], place_ref[2]
    unit = (
        lax.broadcasted_iota(jnp.int32, (128, 128), 0) == lax.broadcasted_iota(jnp.int32, (128, 128), 1)
    ).astype(F32).astype(BF16)
    for o in range(OCC):
        for half in range(2):
            for i, ref in enumerate((own_ref, other_ref)):
                across = lax.dot_general(
                    unit, ref[o, :, half * 128 : half * 128 + 128], (((1,), (1,)), ((), ())), preferred_element_type=F32
                )
                turned[half, pl.ds(o * 128, 128), pl.ds(i * ROWS, ROWS)] = across.astype(BF16)
    product(core, 0, turned, own_ref, other_ref, done)
    for d in range(4):
        for h in range(2):
            which, at = PLACES[d, h]
            for u in range(2):
                for j in range(4):
                    for half in range(2):
                        part = tile(done, half, j, h * 4 + lax.rem(y + d, 4), u)
                        if at is None:
                            outs[which][u, j, half] = part
                        else:
                            outs[which][at, u, j, half] = part


def along_x_kernel(place_ref, own_ref, other_ref, turned, *rest):
    outs, done = rest[:5], rest[5]
    x, core = place_ref[0], place_ref[2]
    product(core, 4, turned, own_ref, other_ref, done)
    for d in range(4):
        to = lax.rem(x + d, 4)
        for h in range(2):
            which, at = PLACES[d, h]
            for u in range(2):
                for j in range(4):
                    for half in range(2):
                        part = tile(done, half, j, to // 2 * 4 + h * 2 + u, lax.rem(to, 2))
                        if at is None:
                            outs[which][u, j, half] = part
                        else:
                            outs[which][at, u, j, half] = part


PART = (4, 2, 64, 128)


def partial(place, own, other):
    pair = jax.ShapeDtypeStruct((2, 2) + PART, BF16)
    single = jax.ShapeDtypeStruct((2,) + PART, BF16)
    outs = [pair, pair, single, single, pair]
    done = pltpu.VMEM((2, 2, OCC, 128, 256), BF16)
    *first, turned = pl.pallas_call(
        along_y_kernel,
        out_shape=outs + [jax.ShapeDtypeStruct((2, OCC * 128, 2 * ROWS), BF16)],
        in_specs=[SMEM, VMEM, VMEM],
        out_specs=[VMEM] * 6,
        scratch_shapes=[done],
        compiler_params=params(32),
    )(place, own, other)
    second = pl.pallas_call(
        along_x_kernel,
        out_shape=outs,
        in_specs=[SMEM, VMEM, VMEM, VMEM],
        out_specs=[VMEM] * 5,
        scratch_shapes=[done],
        compiler_params=params(32),
    )(place, own, other, turned)
    return first, second


def first_sum_kernel(place_ref, own, from_back, from_ahead, last_back, last_ahead, *rest, at):
    outs, kept = rest[:4], rest[4]
    for h, (one, two) in enumerate(((from_ahead, last_back), (from_back, last_ahead))):
        for u in range(2):
            total = own[h, u].astype(F32) + one[1, u].astype(F32) + two[u].astype(F32)
            kept[h * 2 + u] = total.astype(BF16)
    for d in range(4):
        outs[d][...] = kept[lax.rem(place_ref[at] + d, 4)]


def first_sum(place, at, ins):
    def kernel(*refs):
        first_sum_kernel(*refs, at=at)

    return pl.pallas_call(
        kernel,
        out_shape=[jax.ShapeDtypeStruct(PART, BF16)] * 4,
        in_specs=[SMEM] + [VMEM] * 5,
        out_specs=[VMEM] * 4,
        scratch_shapes=[pltpu.VMEM((4,) + PART, BF16)],
        compiler_params=params(16),
    )(place, *ins)


def second_sum_kernel(*refs):
    ins, out = refs[:8], refs[8]
    for half in range(2):
        total = ins[half * 4][...].astype(F32)
        for d in range(1, 4):
            total = total + ins[half * 4 + d][...].astype(F32)
        out[pl.ds(half * 4, 4)] = total


def second_sum(ins):
    return pl.pallas_call(
        second_sum_kernel,
        out_shape=jax.ShapeDtypeStruct((OCC, 2, 64, 128), F32),
        in_specs=[VMEM] * 8,
        out_specs=VMEM,
        compiler_params=params(16),
    )(*ins)


def finish_kernel(place_ref, parts_ref, below_ref, out_ref):
    core, low = place_ref[2], place_ref[3]
    total = parts_ref[0]
    for z in range(1, 8):
        total = total + parts_ref[z]
    across = [total[half].T for half in range(2)]
    crossed = []
    for half in range(2):
        source = jnp.where(core == 0, across[half], across[1 - half])
        same = jnp.concatenate([source[0:64], source[64:128]], axis=1)
        other = jnp.concatenate([source[64:128], source[0:64]], axis=1)
        crossed.append(jnp.where(low == 0, same, other))
    amplitudes = [total[half] / below_ref[half] for half in range(2)]
    terms = [amplitudes[half] * (2.0 * total[half] - crossed[half]) for half in range(2)]
    energy = jnp.sum(terms[0] + terms[1], axis=(0, 1), keepdims=True)
    lane = lax.broadcasted_iota(jnp.int32, (64, 128), 1)
    quarter = lax.rem(lane // 64 + low, 2)
    for half in range(2):
        for q in range(2):
            sent = jnp.where(quarter == q, amplitudes[half], jnp.broadcast_to(energy, (64, 128)))
            out_ref[pl.ds(half * 16 + q * 8, 8)] = sent.reshape(8, 8, 128)


def finish(place, parts, below):
    return pl.pallas_call(
        finish_kernel,
        out_shape=jax.ShapeDtypeStruct((32, 8, 128), F32),
        in_specs=[SMEM, VMEM, VMEM],
        out_specs=VMEM,
        compiler_params=params(16),
    )(place, parts, below)


def collect_kernel(place_ref, parts_ref, amp_ref, pair_ref):
    block = place_ref[4]
    half, quarter = block // 16, lax.rem(block // 8, 2)
    lane = lax.broadcasted_iota(jnp.int32, (8, 128), 1)
    ours = lane // 64 == quarter
    energies = jnp.zeros((8, 128), F32)
    for j in range(OCC):
        rest = jnp.zeros((8, 128), F32)
        for side in range(2):
            core = lax.rem(half + side, 2)
            one, two = parts_ref[j * 4 + core], parts_ref[j * 4 + 2 + core]
            amp = jnp.where(ours, one, two)
            rest = rest + jnp.where(ours, two, one)
            for r in range(8):
                amp_ref[r, pl.ds(j, 1), pl.ds(side * 128, 128)] = amp[r : r + 1, :]
        total = rest[:, 0:1] + rest[:, 64:65]
        energies = jnp.where(lane == j, jnp.broadcast_to(total, (8, 128)), energies)
    pair_ref[...] = energies[0:1, 0:OCC]


def collect(place, parts):
    return pl.pallas_call(
        collect_kernel,
        out_shape=[jax.ShapeDtypeStruct((8, OCC, VIR), F32), jax.ShapeDtypeStruct((1, OCC), F32)],
        in_specs=[SMEM, VMEM],
        out_specs=[VMEM, VMEM],
        compiler_params=params(16),
    )(place, parts)


def moved(x, axis, by):
    n = lax.axis_size(axis)
    return lax.ppermute(x, axis, [(i, (i + by) % n) for i in range(n)])


def denominators(eps_occ, eps_vir, occ_index, core, low):
    levels = jnp.take(eps_occ, occ_index)
    own = jnp.sum(jnp.where(jnp.arange(OCC) == lax.axis_index(AUX), levels, 0.0))
    other = jnp.sum(jnp.where(jnp.arange(OCC) == lax.axis_index("z"), levels, 0.0))
    quarters = eps_vir.reshape(2, 2, 64, 1)
    of_rows = jnp.where((jnp.arange(128) // 64 + low) % 2 == 0, quarters[:, 0], quarters[:, 1])
    halves = eps_vir.reshape(2, 1, 128)
    of_columns = jnp.where(core == 0, halves, halves[::-1])
    return own + other - of_rows - of_columns


def body(three_center, slot_block, slot_aux, live_slots, vir_coef, eps_occ, eps_vir, occ_index):
    x, y, core, low = lax.axis_index(X), lax.axis_index("y"), lax.axis_index("core"), lax.axis_index("xl")
    place = jnp.stack([x, y, core, low, lax.axis_index(BLK)]).astype(jnp.int32)
    own = half_transform(slot_block, slot_aux, live_slots, three_center, vir_coef)
    other = moved(own, "core", 1)
    below = denominators(eps_occ, eps_vir, occ_index, core, low)

    got = []
    for axis, (ahead, back, one, minus, mine) in zip(("y", X), partial(place, own, other)):
        got.append((axis, moved(ahead, axis, 1), moved(back, axis, -1), one, minus, mine))
    ins = []
    for at, (axis, from_back, from_ahead, one, minus, mine) in enumerate(got):
        one = (one.astype(F32) + from_back[0].astype(F32)).astype(BF16)
        minus = (minus.astype(F32) + from_ahead[0].astype(F32)).astype(BF16)
        last = moved(one, axis, 1), moved(minus, axis, -1)
        group = first_sum(place, at, (mine, from_back, from_ahead, *last))
        ins += [group[0]] + [moved(group[d], (X, "y")[at], d) for d in range(1, 4)]
    parts = lax.all_to_all(second_sum(ins), "z", 0, 0, tiled=True)
    sent = finish(place, parts, below)
    amplitudes, pair = collect(place, lax.all_to_all(sent, BLK, 0, 0, tiled=True))
    return amplitudes[None], pair


def solution(mesh):
    fine = Mesh(mesh.devices.reshape(2, 4, 8, 2, 2), ("xh", "y", "z", "xl", "core"))
    every = AUX + BLK
    in_specs = (P(every, None, None, None), P(every), P(every), P(every), P(), P(), P(), P())
    out_specs = (P(AUX, BLK, None, None), P(AUX, None))
    return jax.shard_map(body, mesh=fine, in_specs=in_specs, out_specs=out_specs, check_vma=False)
```

```python
import jax
import jax.numpy as jnp
from jax import lax
from jax.experimental import pallas as pl
from jax.experimental.pallas import tpu as pltpu
from jax.sharding import Mesh
from jax.sharding import PartitionSpec as P

F32 = jnp.float32
BF16 = jnp.bfloat16
OCC = 8
VIR = 256
SPAN = 128
SLOTS = 12
KINDS = 2
ROWS = 256
STEPS = 32000.0
TINY = 1e-37
AUX = ("xh", "y")
BLK = ("z", "xl", "core")
X = ("xh", "xl")

VMEM = pl.BlockSpec(memory_space=pltpu.VMEM)
SMEM = pl.BlockSpec(memory_space=pltpu.SMEM)
HBM = pl.BlockSpec(memory_space=pltpu.HBM)


def params(mib):
    return pltpu.CompilerParams(vmem_limit_bytes=mib * 2**20)


def in_hbm(x):
    return pltpu.with_memory_space_constraint(x, pltpu.HBM)


def half_kernel(block_hbm, kind_hbm, live_hbm, three_ref, coef_ref, out_ref, block_ref, kind_ref, live_ref, three, coef, weights, sems):
    small = [
        pltpu.make_async_copy(here, there, sems.at[3 * SLOTS + i])
        for i, (here, there) in enumerate(((block_hbm, block_ref), (kind_hbm, kind_ref), (live_hbm, live_ref)))
    ]
    for copy in small:
        copy.start()
    large = []
    for half in range(2):
        for s in range(SLOTS):
            rows, columns = pl.ds(half * 4, 4), pl.ds(s * SPAN, SPAN)
            large.append(
                pltpu.make_async_copy(three_ref.at[s, rows], three.at[rows, :, columns], sems.at[(1 + half) * SLOTS + s])
            )
    for copy in large[:SLOTS]:
        copy.start()
    for copy in small:
        copy.wait()
    copies = []
    for s in range(SLOTS):
        first = pl.multiple_of(block_ref[s] * SPAN, SPAN)
        copies.append(pltpu.make_async_copy(coef_ref.at[pl.ds(first, SPAN)], coef.at[s], sems.at[s]))
        copies[s].start()
    for copy in large[SLOTS:]:
        copy.start()
    for s in range(SLOTS):
        copies[s].wait()
        values = coef[s]
        for k in range(KINDS):
            used = jnp.logical_and(kind_ref[s] == k, s < live_ref[0])
            weights[pl.ds(s * SPAN, SPAN), pl.ds(k * VIR, VIR)] = jnp.where(used, values, jnp.zeros_like(values))
    for half in range(2):
        for s in range(SLOTS):
            large[half * SLOTS + s].wait()
        left = three[pl.ds(half * 4, 4)].reshape(4 * SPAN, SLOTS * SPAN)
        done = jnp.dot(left, weights[...], preferred_element_type=F32).astype(BF16)
        for i in range(4):
            for k in range(KINDS):
                out_ref[half * 4 + i, pl.ds(k * SPAN, SPAN), :] = done[i * SPAN : (i + 1) * SPAN, k * VIR : (k + 1) * VIR]


def half_transform(slot_block, slot_aux, live_slots, three_center, vir_coef):
    return pl.pallas_call(
        half_kernel,
        out_shape=jax.ShapeDtypeStruct((OCC, ROWS, VIR), BF16),
        in_specs=[HBM] * 5,
        out_specs=VMEM,
        scratch_shapes=[
            pltpu.SMEM((SLOTS,), jnp.int32),
            pltpu.SMEM((SLOTS,), jnp.int32),
            pltpu.SMEM((1,), jnp.int32),
            pltpu.VMEM((OCC, SPAN, SLOTS * SPAN), BF16),
            pltpu.VMEM((SLOTS, SPAN, VIR), BF16),
            pltpu.VMEM((SLOTS * SPAN, KINDS * VIR), BF16),
            pltpu.SemaphoreType.DMA((3 * SLOTS + 3,)),
        ],
        compiler_params=params(12),
    )(*(in_hbm(x) for x in (slot_block, slot_aux)), live_slots, in_hbm(three_center), in_hbm(vir_coef))


PLACES = {
    (2, 0): (0, 0), (1, 1): (0, 1), (2, 1): (1, 0), (3, 0): (1, 1),
    (1, 0): (2, None), (3, 1): (3, None), (0, 0): (4, 0), (0, 1): (4, 1),
}


def product(core, first_j, turned, own_ref, other_ref, done):
    for half in range(2):
        columns = pl.ds(pl.multiple_of(lax.rem(core + half, 2) * 128, 128), 128)
        for pair in range(2):
            j = first_j + 2 * pair
            right = jnp.concatenate(
                [jnp.concatenate([ref[j + i, :, columns] for ref in (own_ref, other_ref)], axis=0) for i in range(2)],
                axis=1,
            )
            whole = jnp.dot(turned[half], right, preferred_element_type=F32).astype(BF16)
            done[half, pair] = whole.reshape(OCC, 128, 256)


def tile(done, half, j, o, low):
    lane = lax.broadcasted_iota(jnp.int32, (64, 128), 1)
    columns = pl.ds(j % 2 * 128, 128)
    first, second = done[half, j // 2, o, 0:64, columns], done[half, j // 2, o, 64:128, columns]
    return jnp.where(lax.rem(lane // 64 + low, 2) == 0, first.astype(F32), second.astype(F32)).astype(BF16)


def along_y_kernel(place_ref, own_ref, other_ref, *rest):
    outs, turned, done = rest[:5], rest[5], rest[6]
    y, core = place_ref[1], place_ref[2]
    unit = (
        lax.broadcasted_iota(jnp.int32, (128, 128), 0) == lax.broadcasted_iota(jnp.int32, (128, 128), 1)
    ).astype(F32).astype(BF16)
    for o in range(OCC):
        for half in range(2):
            for i, ref in enumerate((own_ref, other_ref)):
                across = lax.dot_general(
                    unit, ref[o, :, half * 128 : half * 128 + 128], (((1,), (1,)), ((), ())), preferred_element_type=F32
                )
                turned[half, pl.ds(o * 128, 128), pl.ds(i * ROWS, ROWS)] = across.astype(BF16)
    product(core, 0, turned, own_ref, other_ref, done)
    for d in range(4):
        for h in range(2):
            which, at = PLACES[d, h]
            for u in range(2):
                for j in range(4):
                    for half in range(2):
                        part = tile(done, half, j, h * 4 + lax.rem(y + d, 4), u)
                        if at is None:
                            outs[which][u, j, half] = part
                        else:
                            outs[which][at, u, j, half] = part


def along_x_kernel(place_ref, own_ref, other_ref, turned, *rest):
    outs, done = rest[:5], rest[5]
    x, core = place_ref[0], place_ref[2]
    product(core, 4, turned, own_ref, other_ref, done)
    for d in range(4):
        to = lax.rem(x + d, 4)
        for h in range(2):
            which, at = PLACES[d, h]
            for u in range(2):
                for j in range(4):
                    for half in range(2):
                        part = tile(done, half, j, to // 2 * 4 + h * 2 + u, lax.rem(to, 2))
                        if at is None:
                            outs[which][u, j, half] = part
                        else:
                            outs[which][at, u, j, half] = part


PART = (4, 2, 64, 128)


def partial(place, own, other):
    pair = jax.ShapeDtypeStruct((2, 2) + PART, BF16)
    single = jax.ShapeDtypeStruct((2,) + PART, BF16)
    outs = [pair, pair, single, single, pair]
    done = pltpu.VMEM((2, 2, OCC, 128, 256), BF16)
    *first, turned = pl.pallas_call(
        along_y_kernel,
        out_shape=outs + [jax.ShapeDtypeStruct((2, OCC * 128, 2 * ROWS), BF16)],
        in_specs=[SMEM, VMEM, VMEM],
        out_specs=[VMEM] * 6,
        scratch_shapes=[done],
        compiler_params=params(10),
    )(place, own, other)
    second = pl.pallas_call(
        along_x_kernel,
        out_shape=outs,
        in_specs=[SMEM, VMEM, VMEM, VMEM],
        out_specs=[VMEM] * 5,
        scratch_shapes=[done],
        compiler_params=params(10),
    )(place, own, other, turned)
    return first, second


def first_sum_kernel(place_ref, own, from_back, from_ahead, last_back, last_ahead, *rest, at):
    outs, kept = rest[:4], rest[4]
    for h, (one, two) in enumerate(((from_ahead, last_back), (from_back, last_ahead))):
        for u in range(2):
            total = own[h, u].astype(F32) + one[1, u].astype(F32) + two[u].astype(F32)
            kept[h * 2 + u] = total.astype(BF16)
    for d in range(4):
        outs[d][...] = kept[lax.rem(place_ref[at] + d, 4)]


def first_sum(place, at, ins):
    def kernel(*refs):
        first_sum_kernel(*refs, at=at)

    return pl.pallas_call(
        kernel,
        out_shape=[jax.ShapeDtypeStruct(PART, BF16)] * 4,
        in_specs=[SMEM] + [VMEM] * 5,
        out_specs=[VMEM] * 4,
        scratch_shapes=[pltpu.VMEM((4,) + PART, BF16)],
        compiler_params=params(6),
    )(place, *ins)


def second_sum_kernel(*refs):
    ins, out = refs[:8], refs[8]
    for half in range(2):
        for j in range(4):
            total = ins[half * 4][j].astype(F32)
            for d in range(1, 4):
                total = total + ins[half * 4 + d][j].astype(F32)
            total = total.reshape(128, 128)
            largest = jnp.max(jnp.abs(total), axis=(0, 1), keepdims=True)
            power = jnp.ceil(jnp.log2(jnp.maximum(largest, TINY)))
            steps = jnp.round(total * jnp.exp2(-power) * STEPS)
            out[half * 4 + j, 0:128] = steps.astype(jnp.int32).astype(jnp.int16)
            out[half * 4 + j, 128:144] = jnp.broadcast_to(power, (16, 128)).astype(jnp.int32).astype(jnp.int16)


def second_sum(ins):
    return pl.pallas_call(
        second_sum_kernel,
        out_shape=jax.ShapeDtypeStruct((OCC, 144, 128), jnp.int16),
        in_specs=[VMEM] * 8,
        out_specs=VMEM,
        compiler_params=params(6),
    )(*ins)


def finish_kernel(place_ref, parts_ref, below_ref, out_ref):
    core, low = place_ref[2], place_ref[3]
    total = jnp.zeros((128, 128), F32)
    for z in range(8):
        power = parts_ref[z, 128:144].astype(jnp.int32).astype(F32)[0:1]
        total = total + parts_ref[z, 0:128].astype(jnp.int32).astype(F32) * (jnp.exp2(power) * (1.0 / STEPS))
    total = total.reshape(2, 64, 128)
    across = [total[half].T for half in range(2)]
    crossed = []
    for half in range(2):
        source = jnp.where(core == 0, across[half], across[1 - half])
        same = jnp.concatenate([source[0:64], source[64:128]], axis=1)
        other = jnp.concatenate([source[64:128], source[0:64]], axis=1)
        crossed.append(jnp.where(low == 0, same, other))
    amplitudes = [total[half] / below_ref[half] for half in range(2)]
    terms = [amplitudes[half] * (2.0 * total[half] - crossed[half]) for half in range(2)]
    energy = jnp.sum(terms[0] + terms[1], axis=(0, 1), keepdims=True)
    lane = lax.broadcasted_iota(jnp.int32, (64, 128), 1)
    quarter = lax.rem(lane // 64 + low, 2)
    for half in range(2):
        for q in range(2):
            sent = jnp.where(quarter == q, amplitudes[half], jnp.broadcast_to(energy, (64, 128)))
            out_ref[pl.ds(half * 16 + q * 8, 8)] = sent.reshape(8, 8, 128)


def finish(place, parts, below):
    return pl.pallas_call(
        finish_kernel,
        out_shape=jax.ShapeDtypeStruct((32, 8, 128), F32),
        in_specs=[SMEM, VMEM, VMEM],
        out_specs=VMEM,
        compiler_params=params(6),
    )(place, parts, below)


def collect_kernel(place_ref, parts_ref, amp_ref, pair_ref):
    block = place_ref[4]
    half, quarter = block // 16, lax.rem(block // 8, 2)
    lane = lax.broadcasted_iota(jnp.int32, (8, 128), 1)
    ours = lane // 64 == quarter
    energies = jnp.zeros((8, 128), F32)
    for j in range(OCC):
        rest = jnp.zeros((8, 128), F32)
        for side in range(2):
            core = lax.rem(half + side, 2)
            one, two = parts_ref[j * 4 + core], parts_ref[j * 4 + 2 + core]
            amp = jnp.where(ours, one, two)
            rest = rest + jnp.where(ours, two, one)
            for r in range(8):
                amp_ref[r, pl.ds(j, 1), pl.ds(side * 128, 128)] = amp[r : r + 1, :]
        total = rest[:, 0:1] + rest[:, 64:65]
        energies = jnp.where(lane == j, jnp.broadcast_to(total, (8, 128)), energies)
    pair_ref[...] = energies[0:1, 0:OCC]


def collect(place, parts):
    return pl.pallas_call(
        collect_kernel,
        out_shape=[jax.ShapeDtypeStruct((8, OCC, VIR), F32), jax.ShapeDtypeStruct((1, OCC), F32)],
        in_specs=[SMEM, VMEM],
        out_specs=[VMEM, VMEM],
        compiler_params=params(6),
    )(place, parts)


def moved(x, axis, by):
    n = lax.axis_size(axis)
    return lax.ppermute(x, axis, [(i, (i + by) % n) for i in range(n)])


def denominators(eps_occ, eps_vir, occ_index, core, low):
    levels = jnp.take(eps_occ, occ_index)
    own = jnp.sum(jnp.where(jnp.arange(OCC) == lax.axis_index(AUX), levels, 0.0))
    other = jnp.sum(jnp.where(jnp.arange(OCC) == lax.axis_index("z"), levels, 0.0))
    quarters = eps_vir.reshape(2, 2, 64, 1)
    of_rows = jnp.where((jnp.arange(128) // 64 + low) % 2 == 0, quarters[:, 0], quarters[:, 1])
    halves = eps_vir.reshape(2, 1, 128)
    of_columns = jnp.where(core == 0, halves, halves[::-1])
    return own + other - of_rows - of_columns


def body(three_center, slot_block, slot_aux, live_slots, vir_coef, eps_occ, eps_vir, occ_index):
    x, y, core, low = lax.axis_index(X), lax.axis_index("y"), lax.axis_index("core"), lax.axis_index("xl")
    place = jnp.stack([x, y, core, low, lax.axis_index(BLK)]).astype(jnp.int32)
    own = half_transform(slot_block, slot_aux, live_slots, three_center, vir_coef)
    other = moved(own, "core", 1)
    below = denominators(eps_occ, eps_vir, occ_index, core, low)
    other, below = lax.optimization_barrier((other, below))

    got = []
    for axis, (ahead, back, one, minus, mine) in zip(("y", X), partial(place, own, other)):
        got.append((axis, moved(ahead, axis, 1), moved(back, axis, -1), one, minus, mine))
    ins = []
    for at, (axis, from_back, from_ahead, one, minus, mine) in enumerate(got):
        one = (one.astype(F32) + from_back[0].astype(F32)).astype(BF16)
        minus = (minus.astype(F32) + from_ahead[0].astype(F32)).astype(BF16)
        last = moved(one, axis, 1), moved(minus, axis, -1)
        group = first_sum(place, at, (mine, from_back, from_ahead, *last))
        ins += [group[0]] + [moved(group[d], (X, "y")[at], d) for d in range(1, 4)]
    parts = lax.all_to_all(second_sum(ins), "z", 0, 0, tiled=True)
    sent = finish(place, parts, below)
    amplitudes, pair = collect(place, lax.all_to_all(sent, BLK, 0, 0, tiled=True))
    return amplitudes[None], pair


def solution(mesh):
    fine = Mesh(mesh.devices.reshape(2, 4, 8, 2, 2), ("xh", "y", "z", "xl", "core"))
    every = AUX + BLK
    in_specs = (P(every, None, None, None), P(every), P(every), P(every), P(), P(), P(), P())
    out_specs = (P(AUX, BLK, None, None), P(AUX, None))
    return jax.shard_map(body, mesh=fine, in_specs=in_specs, out_specs=out_specs, check_vma=False)
```

```python
import jax
import jax.numpy as jnp
from jax import lax
from jax.experimental import pallas as pl
from jax.experimental.pallas import tpu as pltpu
from jax.sharding import Mesh
from jax.sharding import PartitionSpec as P

F32 = jnp.float32
BF16 = jnp.bfloat16
OCC = 8
VIR = 256
SPAN = 128
SLOTS = 12
KINDS = 2
ROWS = 256
STEPS = 32000.0
TINY = 1e-37
AUX = ("xh", "y")
BLK = ("z", "xl", "core")
X = ("xh", "xl")

VMEM = pl.BlockSpec(memory_space=pltpu.VMEM)
SMEM = pl.BlockSpec(memory_space=pltpu.SMEM)
HBM = pl.BlockSpec(memory_space=pltpu.HBM)


def params(mib):
    return pltpu.CompilerParams(vmem_limit_bytes=mib * 2**20)


def in_hbm(x):
    return pltpu.with_memory_space_constraint(x, pltpu.HBM)


def half_kernel(block_hbm, kind_hbm, live_hbm, three_ref, coef_ref, out_ref, block_ref, kind_ref, live_ref, three, coef, weights, sems):
    small = [
        pltpu.make_async_copy(here, there, sems.at[3 * SLOTS + i])
        for i, (here, there) in enumerate(((block_hbm, block_ref), (kind_hbm, kind_ref), (live_hbm, live_ref)))
    ]
    for copy in small:
        copy.start()
    large = []
    for half in range(2):
        for s in range(SLOTS):
            rows, columns = pl.ds(half * 4, 4), pl.ds(s * SPAN, SPAN)
            large.append(
                pltpu.make_async_copy(three_ref.at[s, rows], three.at[rows, :, columns], sems.at[(1 + half) * SLOTS + s])
            )
    for copy in large[:SLOTS]:
        copy.start()
    for copy in small:
        copy.wait()
    copies = []
    for s in range(SLOTS):
        first = pl.multiple_of(block_ref[s] * SPAN, SPAN)
        copies.append(pltpu.make_async_copy(coef_ref.at[pl.ds(first, SPAN)], coef.at[s], sems.at[s]))
        copies[s].start()
    for copy in large[SLOTS:]:
        copy.start()
    for s in range(SLOTS):
        copies[s].wait()
        values = coef[s]
        for k in range(KINDS):
            used = jnp.logical_and(kind_ref[s] == k, s < live_ref[0])
            weights[pl.ds(s * SPAN, SPAN), pl.ds(k * VIR, VIR)] = jnp.where(used, values, jnp.zeros_like(values))
    for half in range(2):
        for s in range(SLOTS):
            large[half * SLOTS + s].wait()
        left = three[pl.ds(half * 4, 4)].reshape(4 * SPAN, SLOTS * SPAN)
        done = jnp.dot(left, weights[...], preferred_element_type=F32).astype(BF16)
        for i in range(4):
            for k in range(KINDS):
                out_ref[half * 4 + i, pl.ds(k * SPAN, SPAN), :] = done[i * SPAN : (i + 1) * SPAN, k * VIR : (k + 1) * VIR]


def half_transform(slot_block, slot_aux, live_slots, three_center, vir_coef):
    return pl.pallas_call(
        half_kernel,
        out_shape=jax.ShapeDtypeStruct((OCC, ROWS, VIR), BF16),
        in_specs=[HBM] * 5,
        out_specs=VMEM,
        scratch_shapes=[
            pltpu.SMEM((SLOTS,), jnp.int32),
            pltpu.SMEM((SLOTS,), jnp.int32),
            pltpu.SMEM((1,), jnp.int32),
            pltpu.VMEM((OCC, SPAN, SLOTS * SPAN), BF16),
            pltpu.VMEM((SLOTS, SPAN, VIR), BF16),
            pltpu.VMEM((SLOTS * SPAN, KINDS * VIR), BF16),
            pltpu.SemaphoreType.DMA((3 * SLOTS + 3,)),
        ],
        compiler_params=params(12),
    )(*(in_hbm(x) for x in (slot_block, slot_aux)), live_slots, in_hbm(three_center), in_hbm(vir_coef))


PLACES = {
    (2, 0): (0, 0), (1, 1): (0, 1), (2, 1): (1, 0), (3, 0): (1, 1),
    (1, 0): (2, None), (3, 1): (3, None), (0, 0): (4, 0), (0, 1): (4, 1),
}


def product(core, first_j, turned, own_ref, other_ref, done):
    left = lax.broadcasted_iota(jnp.int32, (64, 128), 1) < 64
    for half in range(2):
        columns = pl.ds(pl.multiple_of(lax.rem(core + half, 2) * 128, 128), 128)
        for pair in range(2):
            j = first_j + 2 * pair
            right = jnp.concatenate(
                [jnp.concatenate([ref[j + i, :, columns] for ref in (own_ref, other_ref)], axis=0) for i in range(2)],
                axis=1,
            )
            whole = jnp.dot(turned[half], right, preferred_element_type=F32)
            for o in range(OCC):
                for i in range(2):
                    first = whole[o * 128 : o * 128 + 64, i * 128 : i * 128 + 128]
                    second = whole[o * 128 + 64 : o * 128 + 128, i * 128 : i * 128 + 128]
                    done[half, 2 * pair + i, o, 0] = jnp.where(left, first, second).astype(BF16)
                    done[half, 2 * pair + i, o, 1] = jnp.where(left, second, first).astype(BF16)


def along_y_kernel(place_ref, own_ref, other_ref, *rest):
    outs, turned, done = rest[:5], rest[5], rest[6]
    y, core = place_ref[1], place_ref[2]
    unit = (
        lax.broadcasted_iota(jnp.int32, (128, 128), 0) == lax.broadcasted_iota(jnp.int32, (128, 128), 1)
    ).astype(F32).astype(BF16)
    for o in range(OCC):
        for half in range(2):
            for i, ref in enumerate((own_ref, other_ref)):
                across = lax.dot_general(
                    unit, ref[o, :, half * 128 : half * 128 + 128], (((1,), (1,)), ((), ())), preferred_element_type=F32
                )
                turned[half, pl.ds(o * 128, 128), pl.ds(i * ROWS, ROWS)] = across.astype(BF16)
    product(core, 0, turned, own_ref, other_ref, done)
    for d in range(4):
        for h in range(2):
            which, at = PLACES[d, h]
            for u in range(2):
                for j in range(4):
                    for half in range(2):
                        part = done[half, j, h * 4 + lax.rem(y + d, 4), u]
                        if at is None:
                            outs[which][u, j, half] = part
                        else:
                            outs[which][at, u, j, half] = part


def along_x_kernel(place_ref, own_ref, other_ref, turned, *rest):
    outs, done = rest[:5], rest[5]
    x, core = place_ref[0], place_ref[2]
    product(core, 4, turned, own_ref, other_ref, done)
    for d in range(4):
        to = lax.rem(x + d, 4)
        for h in range(2):
            which, at = PLACES[d, h]
            for u in range(2):
                for j in range(4):
                    for half in range(2):
                        part = done[half, j, to // 2 * 4 + h * 2 + u, lax.rem(to, 2)]
                        if at is None:
                            outs[which][u, j, half] = part
                        else:
                            outs[which][at, u, j, half] = part


PART = (4, 2, 64, 128)


def partial(place, own, other):
    pair = jax.ShapeDtypeStruct((2, 2) + PART, BF16)
    single = jax.ShapeDtypeStruct((2,) + PART, BF16)
    outs = [pair, pair, single, single, pair]
    done = pltpu.VMEM((2, 4, OCC, 2, 64, 128), BF16)
    *first, turned = pl.pallas_call(
        along_y_kernel,
        out_shape=outs + [jax.ShapeDtypeStruct((2, OCC * 128, 2 * ROWS), BF16)],
        in_specs=[SMEM, VMEM, VMEM],
        out_specs=[VMEM] * 6,
        scratch_shapes=[done],
        compiler_params=params(10),
    )(place, own, other)
    second = pl.pallas_call(
        along_x_kernel,
        out_shape=outs,
        in_specs=[SMEM, VMEM, VMEM, VMEM],
        out_specs=[VMEM] * 5,
        scratch_shapes=[done],
        compiler_params=params(10),
    )(place, own, other, turned)
    return first, second


def first_sum_kernel(place_ref, own, from_back, from_ahead, last_back, last_ahead, *outs, at):
    for d in range(4):
        to = lax.rem(place_ref[at] + d, 4)
        h, u = to // 2, lax.rem(to, 2)
        for side, (one, two) in enumerate(((from_ahead, last_back), (from_back, last_ahead))):

            @pl.when(h == side)
            def _():
                total = own[side, u].astype(F32) + one[1, u].astype(F32) + two[u].astype(F32)
                outs[d][...] = total.astype(BF16)


def first_sum(place, at, ins):
    def kernel(*refs):
        first_sum_kernel(*refs, at=at)

    return pl.pallas_call(
        kernel,
        out_shape=[jax.ShapeDtypeStruct(PART, BF16)] * 4,
        in_specs=[SMEM] + [VMEM] * 5,
        out_specs=[VMEM] * 4,
        compiler_params=params(6),
    )(place, *ins)


def second_sum_kernel(*refs):
    ins, out = refs[:8], refs[8]
    for half in range(2):
        for j in range(4):
            total = ins[half * 4][j].astype(F32)
            for d in range(1, 4):
                total = total + ins[half * 4 + d][j].astype(F32)
            total = total.reshape(128, 128)
            largest = jnp.max(jnp.abs(total), axis=(0, 1), keepdims=True)
            power = jnp.ceil(jnp.log2(jnp.maximum(largest, TINY)))
            steps = jnp.round(total * jnp.exp2(-power) * STEPS)
            out[half * 4 + j, 0:128] = steps.astype(jnp.int32).astype(jnp.int16)
            out[half * 4 + j, 128:144] = jnp.broadcast_to(power, (16, 128)).astype(jnp.int32).astype(jnp.int16)


def second_sum(ins):
    return pl.pallas_call(
        second_sum_kernel,
        out_shape=jax.ShapeDtypeStruct((OCC, 144, 128), jnp.int16),
        in_specs=[VMEM] * 8,
        out_specs=VMEM,
        compiler_params=params(6),
    )(*ins)


def finish_kernel(place_ref, parts_ref, below_ref, out_ref):
    core, low = place_ref[2], place_ref[3]
    total = jnp.zeros((128, 128), F32)
    for z in range(8):
        power = parts_ref[z, 128:144].astype(jnp.int32).astype(F32)[0:1]
        total = total + parts_ref[z, 0:128].astype(jnp.int32).astype(F32) * (jnp.exp2(power) * (1.0 / STEPS))
    total = total.reshape(2, 64, 128)
    across = [total[half].T for half in range(2)]
    crossed = []
    for half in range(2):
        source = jnp.where(core == 0, across[half], across[1 - half])
        same = jnp.concatenate([source[0:64], source[64:128]], axis=1)
        other = jnp.concatenate([source[64:128], source[0:64]], axis=1)
        crossed.append(jnp.where(low == 0, same, other))
    amplitudes = [total[half] / below_ref[half] for half in range(2)]
    terms = [amplitudes[half] * (2.0 * total[half] - crossed[half]) for half in range(2)]
    energy = jnp.sum(terms[0] + terms[1], axis=(0, 1), keepdims=True)
    lane = lax.broadcasted_iota(jnp.int32, (64, 128), 1)
    quarter = lax.rem(lane // 64 + low, 2)
    for half in range(2):
        for q in range(2):
            sent = jnp.where(quarter == q, amplitudes[half], jnp.broadcast_to(energy, (64, 128)))
            out_ref[pl.ds(half * 16 + q * 8, 8)] = sent.reshape(8, 8, 128)


def finish(place, parts, below):
    return pl.pallas_call(
        finish_kernel,
        out_shape=jax.ShapeDtypeStruct((32, 8, 128), F32),
        in_specs=[SMEM, VMEM, VMEM],
        out_specs=VMEM,
        compiler_params=params(6),
    )(place, parts, below)


def collect_kernel(place_ref, parts_ref, amp_ref, pair_ref):
    block = place_ref[4]
    half, quarter = block // 16, lax.rem(block // 8, 2)
    lane = lax.broadcasted_iota(jnp.int32, (8, 128), 1)
    ours = lane // 64 == quarter
    energies = jnp.zeros((8, 128), F32)
    for j in range(OCC):
        rest = jnp.zeros((8, 128), F32)
        for side in range(2):
            core = lax.rem(half + side, 2)
            one, two = parts_ref[j * 4 + core], parts_ref[j * 4 + 2 + core]
            amp = jnp.where(ours, one, two)
            rest = rest + jnp.where(ours, two, one)
            for r in range(8):
                amp_ref[r, pl.ds(j, 1), pl.ds(side * 128, 128)] = amp[r : r + 1, :]
        total = rest[:, 0:1] + rest[:, 64:65]
        energies = jnp.where(lane == j, jnp.broadcast_to(total, (8, 128)), energies)
    pair_ref[...] = energies[0:1, 0:OCC]


def collect(place, parts):
    return pl.pallas_call(
        collect_kernel,
        out_shape=[jax.ShapeDtypeStruct((8, OCC, VIR), F32), jax.ShapeDtypeStruct((1, OCC), F32)],
        in_specs=[SMEM, VMEM],
        out_specs=[VMEM, VMEM],
        compiler_params=params(6),
    )(place, parts)


def moved(x, axis, by):
    n = lax.axis_size(axis)
    return lax.ppermute(x, axis, [(i, (i + by) % n) for i in range(n)])


def denominators(eps_occ, eps_vir, occ_index, core, low):
    levels = jnp.take(eps_occ, occ_index)
    own = jnp.sum(jnp.where(jnp.arange(OCC) == lax.axis_index(AUX), levels, 0.0))
    other = jnp.sum(jnp.where(jnp.arange(OCC) == lax.axis_index("z"), levels, 0.0))
    quarters = eps_vir.reshape(2, 2, 64, 1)
    of_rows = jnp.where((jnp.arange(128) // 64 + low) % 2 == 0, quarters[:, 0], quarters[:, 1])
    halves = eps_vir.reshape(2, 1, 128)
    of_columns = jnp.where(core == 0, halves, halves[::-1])
    return own + other - of_rows - of_columns


def body(three_center, slot_block, slot_aux, live_slots, vir_coef, eps_occ, eps_vir, occ_index):
    x, y, core, low = lax.axis_index(X), lax.axis_index("y"), lax.axis_index("core"), lax.axis_index("xl")
    place = jnp.stack([x, y, core, low, lax.axis_index(BLK)]).astype(jnp.int32)
    own = half_transform(slot_block, slot_aux, live_slots, three_center, vir_coef)
    other = moved(own, "core", 1)
    below = denominators(eps_occ, eps_vir, occ_index, core, low)
    other, below = lax.optimization_barrier((other, below))

    got = []
    for axis, (ahead, back, one, minus, mine) in zip(("y", X), partial(place, own, other)):
        got.append((axis, moved(ahead, axis, 1), moved(back, axis, -1), one, minus, mine))
    ins = []
    for at, (axis, from_back, from_ahead, one, minus, mine) in enumerate(got):
        one = (one.astype(F32) + from_back[0].astype(F32)).astype(BF16)
        minus = (minus.astype(F32) + from_ahead[0].astype(F32)).astype(BF16)
        last = moved(one, axis, 1), moved(minus, axis, -1)
        group = first_sum(place, at, (mine, from_back, from_ahead, *last))
        ins += [group[0]] + [moved(group[d], (X, "y")[at], d) for d in (2, 1, 3)]
    parts = lax.all_to_all(second_sum(ins), "z", 0, 0, tiled=True)
    sent = finish(place, parts, below)
    amplitudes, pair = collect(place, lax.all_to_all(sent, BLK, 0, 0, tiled=True))
    return amplitudes[None], pair


def solution(mesh):
    fine = Mesh(mesh.devices.reshape(2, 4, 8, 2, 2), ("xh", "y", "z", "xl", "core"))
    every = AUX + BLK
    in_specs = (P(every, None, None, None), P(every), P(every), P(every), P(), P(), P(), P())
    out_specs = (P(AUX, BLK, None, None), P(AUX, None))
    return jax.shard_map(body, mesh=fine, in_specs=in_specs, out_specs=out_specs, check_vma=False)
```

```python
import jax
import jax.numpy as jnp
from jax import lax
from jax.experimental import pallas as pl
from jax.experimental.pallas import tpu as pltpu
from jax.sharding import Mesh
from jax.sharding import PartitionSpec as P

F32 = jnp.float32
BF16 = jnp.bfloat16
OCC = 8
VIR = 256
SPAN = 128
SLOTS = 12
KINDS = 2
ROWS = 256
STEPS = 32000.0
TINY = 1e-37
AUX = ("xh", "y")
BLK = ("z", "xl", "core")
X = ("xh", "xl")

VMEM = pl.BlockSpec(memory_space=pltpu.VMEM)
SMEM = pl.BlockSpec(memory_space=pltpu.SMEM)
HBM = pl.BlockSpec(memory_space=pltpu.HBM)


def params(mib):
    return pltpu.CompilerParams(vmem_limit_bytes=mib * 2**20)


def in_hbm(x):
    return pltpu.with_memory_space_constraint(x, pltpu.HBM)


def half_kernel(block_hbm, kind_hbm, live_hbm, three_ref, coef_ref, out_ref, block_ref, kind_ref, live_ref, three, coef, weights, sems):
    small = [
        pltpu.make_async_copy(here, there, sems.at[3 * SLOTS + i])
        for i, (here, there) in enumerate(((block_hbm, block_ref), (kind_hbm, kind_ref), (live_hbm, live_ref)))
    ]
    for copy in small:
        copy.start()
    large = []
    for half in range(2):
        for s in range(SLOTS):
            rows, columns = pl.ds(half * 4, 4), pl.ds(s * SPAN, SPAN)
            large.append(
                pltpu.make_async_copy(three_ref.at[s, rows], three.at[rows, :, columns], sems.at[(1 + half) * SLOTS + s])
            )
    for copy in large[:SLOTS]:
        copy.start()
    for copy in small:
        copy.wait()
    copies = []
    for s in range(SLOTS):
        first = pl.multiple_of(block_ref[s] * SPAN, SPAN)
        copies.append(pltpu.make_async_copy(coef_ref.at[pl.ds(first, SPAN)], coef.at[s], sems.at[s]))
        copies[s].start()
    for copy in large[SLOTS:]:
        copy.start()
    for s in range(SLOTS):
        copies[s].wait()
        values = coef[s]
        for k in range(KINDS):
            used = jnp.logical_and(kind_ref[s] == k, s < live_ref[0])
            weights[pl.ds(s * SPAN, SPAN), pl.ds(k * VIR, VIR)] = jnp.where(used, values, jnp.zeros_like(values))
    for half in range(2):
        for s in range(SLOTS):
            large[half * SLOTS + s].wait()
        left = three[pl.ds(half * 4, 4)].reshape(4 * SPAN, SLOTS * SPAN)
        done = jnp.dot(left, weights[...], preferred_element_type=F32).astype(BF16)
        for i in range(4):
            for k in range(KINDS):
                out_ref[half * 4 + i, pl.ds(k * SPAN, SPAN), :] = done[i * SPAN : (i + 1) * SPAN, k * VIR : (k + 1) * VIR]


def half_transform(slot_block, slot_aux, live_slots, three_center, vir_coef):
    return pl.pallas_call(
        half_kernel,
        out_shape=jax.ShapeDtypeStruct((OCC, ROWS, VIR), BF16),
        in_specs=[HBM] * 5,
        out_specs=VMEM,
        scratch_shapes=[
            pltpu.SMEM((SLOTS,), jnp.int32),
            pltpu.SMEM((SLOTS,), jnp.int32),
            pltpu.SMEM((1,), jnp.int32),
            pltpu.VMEM((OCC, SPAN, SLOTS * SPAN), BF16),
            pltpu.VMEM((SLOTS, SPAN, VIR), BF16),
            pltpu.VMEM((SLOTS * SPAN, KINDS * VIR), BF16),
            pltpu.SemaphoreType.DMA((3 * SLOTS + 3,)),
        ],
        compiler_params=params(12),
    )(*(in_hbm(x) for x in (slot_block, slot_aux)), live_slots, in_hbm(three_center), in_hbm(vir_coef))


PLACES = {
    (2, 0): (0, 0), (1, 1): (0, 1), (2, 1): (1, 0), (3, 0): (1, 1),
    (1, 0): (2, None), (3, 1): (3, None), (0, 0): (4, 0), (0, 1): (4, 1),
}


def product(core, first_j, turned, own_ref, other_ref, done):
    left = lax.broadcasted_iota(jnp.int32, (64, 128), 1) < 64
    for half in range(2):
        columns = pl.ds(pl.multiple_of(lax.rem(core + half, 2) * 128, 128), 128)
        for pair in range(2):
            j = first_j + 2 * pair
            right = jnp.concatenate(
                [jnp.concatenate([ref[j + i, :, columns] for ref in (own_ref, other_ref)], axis=0) for i in range(2)],
                axis=1,
            )
            whole = jnp.dot(turned[half], right, preferred_element_type=F32)
            for o in range(OCC):
                for i in range(2):
                    first = whole[o * 128 : o * 128 + 64, i * 128 : i * 128 + 128]
                    second = whole[o * 128 + 64 : o * 128 + 128, i * 128 : i * 128 + 128]
                    done[half, 2 * pair + i, o, 0] = jnp.where(left, first, second).astype(BF16)
                    done[half, 2 * pair + i, o, 1] = jnp.where(left, second, first).astype(BF16)


def along_y_kernel(place_ref, own_ref, other_ref, *rest):
    outs, turned, done = rest[:5], rest[5], rest[6]
    y, core = place_ref[1], place_ref[2]
    unit = (
        lax.broadcasted_iota(jnp.int32, (128, 128), 0) == lax.broadcasted_iota(jnp.int32, (128, 128), 1)
    ).astype(F32).astype(BF16)
    for o in range(OCC):
        for half in range(2):
            for i, ref in enumerate((own_ref, other_ref)):
                across = lax.dot_general(
                    unit, ref[o, :, half * 128 : half * 128 + 128], (((1,), (1,)), ((), ())), preferred_element_type=F32
                )
                turned[half, pl.ds(o * 128, 128), pl.ds(i * ROWS, ROWS)] = across.astype(BF16)
    product(core, 0, turned, own_ref, other_ref, done)
    for d in range(4):
        for h in range(2):
            which, at = PLACES[d, h]
            for u in range(2):
                for j in range(4):
                    for half in range(2):
                        part = done[half, j, h * 4 + lax.rem(y + d, 4), u]
                        if at is None:
                            outs[which][u, j, half] = part
                        else:
                            outs[which][at, u, j, half] = part


def along_x_kernel(place_ref, own_ref, other_ref, turned, *rest):
    outs, done = rest[:5], rest[5]
    x, core = place_ref[0], place_ref[2]
    product(core, 4, turned, own_ref, other_ref, done)
    for d in range(4):
        to = lax.rem(x + d, 4)
        for h in range(2):
            which, at = PLACES[d, h]
            for u in range(2):
                for j in range(4):
                    for half in range(2):
                        part = done[half, j, to // 2 * 4 + h * 2 + u, lax.rem(to, 2)]
                        if at is None:
                            outs[which][u, j, half] = part
                        else:
                            outs[which][at, u, j, half] = part


PART = (4, 2, 64, 128)


def partial(place, own, other):
    pair = jax.ShapeDtypeStruct((2, 2) + PART, BF16)
    single = jax.ShapeDtypeStruct((2,) + PART, BF16)
    outs = [pair, pair, single, single, pair]
    done = pltpu.VMEM((2, 4, OCC, 2, 64, 128), BF16)
    *first, turned = pl.pallas_call(
        along_y_kernel,
        out_shape=outs + [jax.ShapeDtypeStruct((2, OCC * 128, 2 * ROWS), BF16)],
        in_specs=[SMEM, VMEM, VMEM],
        out_specs=[VMEM] * 6,
        scratch_shapes=[done],
        compiler_params=params(10),
    )(place, own, other)
    second = pl.pallas_call(
        along_x_kernel,
        out_shape=outs,
        in_specs=[SMEM, VMEM, VMEM, VMEM],
        out_specs=[VMEM] * 5,
        scratch_shapes=[done],
        compiler_params=params(10),
    )(place, own, other, turned)
    return first, second


def first_sum_kernel(place_ref, own, from_back, from_ahead, last_back, last_ahead, *outs, at):
    for d in range(4):
        to = lax.rem(place_ref[at] + d, 4)
        h, u = to // 2, lax.rem(to, 2)
        for side, (one, two) in enumerate(((from_ahead, last_back), (from_back, last_ahead))):

            @pl.when(h == side)
            def _():
                total = own[side, u].astype(F32) + one[1, u].astype(F32) + two[u].astype(F32)
                outs[d][...] = total.astype(BF16)


def first_sum(place, at, ins):
    def kernel(*refs):
        first_sum_kernel(*refs, at=at)

    return pl.pallas_call(
        kernel,
        out_shape=[jax.ShapeDtypeStruct(PART, BF16)] * 4,
        in_specs=[SMEM] + [VMEM] * 5,
        out_specs=[VMEM] * 4,
        compiler_params=params(6),
    )(place, *ins)


def largest(x):
    return jnp.max(jnp.abs(x), axis=(0, 1), keepdims=True)


def power_above(x):
    return jnp.ceil(jnp.log2(jnp.maximum(x, TINY)))


def second_sum_kernel(*refs):
    ins, out = refs[:8], refs[8]
    for half in range(2):
        for j in range(4):
            total = ins[half * 4][j].astype(F32)
            for d in range(1, 4):
                total = total + ins[half * 4 + d][j].astype(F32)
            total = total.reshape(128, 128)
            power = power_above(largest(total))
            steps = jnp.round(total * jnp.exp2(-power) * STEPS)
            out[half * 4 + j, 0:128] = steps.astype(jnp.int32).astype(jnp.int16)
            out[half * 4 + j, 128:144] = jnp.broadcast_to(power, (16, 128)).astype(jnp.int32).astype(jnp.int16)


def second_sum(ins):
    return pl.pallas_call(
        second_sum_kernel,
        out_shape=jax.ShapeDtypeStruct((OCC, 144, 128), jnp.int16),
        in_specs=[VMEM] * 8,
        out_specs=VMEM,
        compiler_params=params(6),
    )(*ins)


def finish_kernel(place_ref, parts_ref, below_ref, out_ref):
    core, low = place_ref[2], place_ref[3]
    total = jnp.zeros((128, 128), F32)
    for z in range(8):
        power = parts_ref[z, 128:144].astype(jnp.int32).astype(F32)[0:1]
        total = total + parts_ref[z, 0:128].astype(jnp.int32).astype(F32) * (jnp.exp2(power) * (1.0 / STEPS))
    total = total.reshape(2, 64, 128)
    across = [total[half].T for half in range(2)]
    crossed = []
    for half in range(2):
        source = jnp.where(core == 0, across[half], across[1 - half])
        same = jnp.concatenate([source[0:64], source[64:128]], axis=1)
        other = jnp.concatenate([source[64:128], source[0:64]], axis=1)
        crossed.append(jnp.where(low == 0, same, other))
    amplitudes = [total[half] / below_ref[half] for half in range(2)]
    terms = [amplitudes[half] * (2.0 * total[half] - crossed[half]) for half in range(2)]
    energy = jnp.sum(terms[0] + terms[1], axis=(0, 1), keepdims=True)
    power = power_above(jnp.maximum(largest(amplitudes[0]), largest(amplitudes[1])))
    power_energy = power_above(jnp.abs(energy))
    scaled = energy * jnp.exp2(-power_energy) * STEPS
    high = jnp.round(scaled)
    lane = lax.broadcasted_iota(jnp.int32, (64, 128), 1)
    which = lax.rem(lane, 4)
    rest = jnp.where(which == 2, high, jnp.round((scaled - high) * STEPS))
    rest = jnp.where(which == 0, power, jnp.where(which == 1, power_energy, rest))
    quarter = lax.rem(lane // 64 + low, 2)
    for half in range(2):
        coded = jnp.round(amplitudes[half] * jnp.exp2(-power) * STEPS)
        for q in range(2):
            sent = jnp.where(quarter == q, coded, rest).astype(jnp.int32).reshape(8, 8, 128)
            out_ref[pl.ds(half * 16 + q * 8, 8)] = sent.astype(jnp.int16)


def finish(place, parts, below):
    return pl.pallas_call(
        finish_kernel,
        out_shape=jax.ShapeDtypeStruct((32, 8, 128), jnp.int16),
        in_specs=[SMEM, VMEM, VMEM],
        out_specs=VMEM,
        compiler_params=params(6),
    )(place, parts, below)


def collect_kernel(place_ref, parts_ref, amp_ref, pair_ref):
    block = place_ref[4]
    half, quarter = block // 16, lax.rem(block // 8, 2)
    lane = lax.broadcasted_iota(jnp.int32, (8, 128), 1)
    ours = lane // 64 == quarter
    coded, rests = [], []
    for j in range(OCC):
        for side in range(2):
            core = lax.rem(half + side, 2)
            one, two = (parts_ref[j * 4 + low * 2 + core].astype(jnp.int32).astype(F32) for low in range(2))
            coded.append(jnp.where(ours, one, two))
            rests.append(jnp.where(ours, two, one)[0:1])
    rest = jnp.concatenate(rests, axis=0)
    first = lax.broadcasted_iota(jnp.int32, (2 * OCC, 128), 1) < 64
    scale = jnp.where(first, jnp.exp2(rest[:, 64:65]), jnp.exp2(rest[:, 0:1])) * (1.0 / STEPS)
    shares = jnp.zeros((2 * OCC, 1), F32)
    for at in (0, 64):
        number = (rest[:, at + 2 : at + 3] + rest[:, at + 3 : at + 4] * (1.0 / STEPS)) * (1.0 / STEPS)
        shares = shares + number * jnp.exp2(rest[:, at + 1 : at + 2])
    energies = jnp.zeros((8, 128), F32)
    for j in range(OCC):
        for side in range(2):
            k = 2 * j + side
            amp = coded[k] * scale[k : k + 1]
            for r in range(8):
                amp_ref[r, pl.ds(j, 1), pl.ds(side * 128, 128)] = amp[r : r + 1, :]
        total = shares[2 * j : 2 * j + 1] + shares[2 * j + 1 : 2 * j + 2]
        energies = jnp.where(lane == j, jnp.broadcast_to(total, (8, 128)), energies)
    pair_ref[...] = energies[0:1, 0:OCC]


def collect(place, parts):
    return pl.pallas_call(
        collect_kernel,
        out_shape=[jax.ShapeDtypeStruct((8, OCC, VIR), F32), jax.ShapeDtypeStruct((1, OCC), F32)],
        in_specs=[SMEM, VMEM],
        out_specs=[VMEM, VMEM],
        compiler_params=params(6),
    )(place, parts)


def moved(x, axis, by):
    n = lax.axis_size(axis)
    return lax.ppermute(x, axis, [(i, (i + by) % n) for i in range(n)])


def denominators(eps_occ, eps_vir, occ_index, core, low):
    levels = jnp.take(eps_occ, occ_index)
    own = jnp.sum(jnp.where(jnp.arange(OCC) == lax.axis_index(AUX), levels, 0.0))
    other = jnp.sum(jnp.where(jnp.arange(OCC) == lax.axis_index("z"), levels, 0.0))
    quarters = eps_vir.reshape(2, 2, 64, 1)
    of_rows = jnp.where((jnp.arange(128) // 64 + low) % 2 == 0, quarters[:, 0], quarters[:, 1])
    halves = eps_vir.reshape(2, 1, 128)
    of_columns = jnp.where(core == 0, halves, halves[::-1])
    return own + other - of_rows - of_columns


def body(three_center, slot_block, slot_aux, live_slots, vir_coef, eps_occ, eps_vir, occ_index):
    x, y, core, low = lax.axis_index(X), lax.axis_index("y"), lax.axis_index("core"), lax.axis_index("xl")
    place = jnp.stack([x, y, core, low, lax.axis_index(BLK)]).astype(jnp.int32)
    own = half_transform(slot_block, slot_aux, live_slots, three_center, vir_coef)
    other = moved(own, "core", 1)
    below = denominators(eps_occ, eps_vir, occ_index, core, low)
    other, below = lax.optimization_barrier((other, below))

    got = []
    for axis, (ahead, back, one, minus, mine) in zip(("y", X), partial(place, own, other)):
        got.append((axis, moved(ahead, axis, 1), moved(back, axis, -1), one, minus, mine))
    ins = []
    for at, (axis, from_back, from_ahead, one, minus, mine) in enumerate(got):
        one = (one.astype(F32) + from_back[0].astype(F32)).astype(BF16)
        minus = (minus.astype(F32) + from_ahead[0].astype(F32)).astype(BF16)
        last = moved(one, axis, 1), moved(minus, axis, -1)
        group = first_sum(place, at, (mine, from_back, from_ahead, *last))
        ins += [group[0]] + [moved(group[d], (X, "y")[at], d) for d in (2, 1, 3)]
    parts = lax.all_to_all(second_sum(ins), "z", 0, 0, tiled=True)
    sent = finish(place, parts, below)
    amplitudes, pair = collect(place, lax.all_to_all(sent, BLK, 0, 0, tiled=True))
    return amplitudes[None], pair


def solution(mesh):
    fine = Mesh(mesh.devices.reshape(2, 4, 8, 2, 2), ("xh", "y", "z", "xl", "core"))
    every = AUX + BLK
    in_specs = (P(every, None, None, None), P(every), P(every), P(every), P(), P(), P(), P())
    out_specs = (P(AUX, BLK, None, None), P(AUX, None))
    return jax.shard_map(body, mesh=fine, in_specs=in_specs, out_specs=out_specs, check_vma=False)
```

```python
import jax
import jax.numpy as jnp
from jax import lax
from jax.experimental import pallas as pl
from jax.experimental.pallas import tpu as pltpu
from jax.sharding import Mesh
from jax.sharding import PartitionSpec as P

F32 = jnp.float32
BF16 = jnp.bfloat16
OCC = 8
VIR = 256
SPAN = 128
SLOTS = 12
KINDS = 2
ROWS = 256
STEPS = 32000.0
TINY = 1e-37
AUX = ("xh", "y")
BLK = ("z", "xl", "core")
X = ("xh", "xl")

VMEM = pl.BlockSpec(memory_space=pltpu.VMEM)
SMEM = pl.BlockSpec(memory_space=pltpu.SMEM)
HBM = pl.BlockSpec(memory_space=pltpu.HBM)


def params(mib):
    return pltpu.CompilerParams(vmem_limit_bytes=mib * 2**20)


def in_hbm(x):
    return pltpu.with_memory_space_constraint(x, pltpu.HBM)


def half_kernel(block_hbm, kind_hbm, live_hbm, three_ref, coef_ref, out_ref, weights, later, block_ref, kind_ref, live_ref, three, coef, sems):
    small = [
        pltpu.make_async_copy(here, there, sems.at[3 * SLOTS + i])
        for i, (here, there) in enumerate(((block_hbm, block_ref), (kind_hbm, kind_ref), (live_hbm, live_ref)))
    ]
    for copy in small:
        copy.start()
    large = []
    for half in range(2):
        for s in range(SLOTS):
            rows, columns = pl.ds(half * 4, 4), pl.ds(s * SPAN, SPAN)
            large.append(
                pltpu.make_async_copy(three_ref.at[s, rows], (three, later)[half].at[:, :, columns], sems.at[(1 + half) * SLOTS + s])
            )
    for copy in large[:SLOTS]:
        copy.start()
    for copy in small:
        copy.wait()
    copies = []
    for s in range(SLOTS):
        first = pl.multiple_of(block_ref[s] * SPAN, SPAN)
        copies.append(pltpu.make_async_copy(coef_ref.at[pl.ds(first, SPAN)], coef.at[s], sems.at[s]))
        copies[s].start()
    for copy in large[SLOTS:]:
        copy.start()
    for s in range(SLOTS):
        copies[s].wait()
        values = coef[s]
        for k in range(KINDS):
            used = jnp.logical_and(kind_ref[s] == k, s < live_ref[0])
            weights[pl.ds(s * SPAN, SPAN), pl.ds(k * VIR, VIR)] = jnp.where(used, values, jnp.zeros_like(values))
    for copy in large[:SLOTS]:
        copy.wait()
    four_rows(three, weights, out_ref)
    for copy in large[SLOTS:]:
        copy.wait()


def four_rows(three, weights, out_ref):
    left = three[...].reshape(4 * SPAN, SLOTS * SPAN)
    done = jnp.dot(left, weights[...], preferred_element_type=F32).astype(BF16)
    for i in range(4):
        for k in range(KINDS):
            out_ref[i, pl.ds(k * SPAN, SPAN), :] = done[i * SPAN : (i + 1) * SPAN, k * VIR : (k + 1) * VIR]


def half_transform(slot_block, slot_aux, live_slots, three_center, vir_coef):
    return pl.pallas_call(
        half_kernel,
        out_shape=[
            jax.ShapeDtypeStruct((4, ROWS, VIR), BF16),
            jax.ShapeDtypeStruct((SLOTS * SPAN, KINDS * VIR), BF16),
            jax.ShapeDtypeStruct((4, SPAN, SLOTS * SPAN), BF16),
        ],
        in_specs=[HBM] * 5,
        out_specs=[VMEM] * 3,
        scratch_shapes=[
            pltpu.SMEM((SLOTS,), jnp.int32),
            pltpu.SMEM((SLOTS,), jnp.int32),
            pltpu.SMEM((1,), jnp.int32),
            pltpu.VMEM((4, SPAN, SLOTS * SPAN), BF16),
            pltpu.VMEM((SLOTS, SPAN, VIR), BF16),
            pltpu.SemaphoreType.DMA((3 * SLOTS + 3,)),
        ],
        compiler_params=params(12),
    )(*(in_hbm(x) for x in (slot_block, slot_aux)), live_slots, in_hbm(three_center), in_hbm(vir_coef))


def other_half(later, weights):
    return pl.pallas_call(
        four_rows,
        out_shape=jax.ShapeDtypeStruct((4, ROWS, VIR), BF16),
        in_specs=[VMEM] * 2,
        out_specs=VMEM,
        compiler_params=params(10),
        cost_estimate=pl.CostEstimate(flops=2 * 512 * 1536 * 512, bytes_accessed=4 * 2**20, transcendentals=0),
    )(later, weights)


PLACES = {
    (2, 0): (0, 0), (1, 1): (0, 1), (2, 1): (1, 0), (3, 0): (1, 1),
    (1, 0): (2, None), (3, 1): (3, None), (0, 0): (4, 0), (0, 1): (4, 1),
}


def product(core, turned, own_ref, other_ref, done):
    left = lax.broadcasted_iota(jnp.int32, (64, 128), 1) < 64
    for half in range(2):
        columns = pl.ds(pl.multiple_of(lax.rem(core + half, 2) * 128, 128), 128)
        for pair in range(2):
            j = 2 * pair
            right = jnp.concatenate(
                [jnp.concatenate([ref[j + i, :, columns] for ref in (own_ref, other_ref)], axis=0) for i in range(2)],
                axis=1,
            )
            whole = jnp.dot(turned[half], right, preferred_element_type=F32)
            for o in range(OCC):
                for i in range(2):
                    first = whole[o * 128 : o * 128 + 64, i * 128 : i * 128 + 128]
                    second = whole[o * 128 + 64 : o * 128 + 128, i * 128 : i * 128 + 128]
                    done[half, 2 * pair + i, o, 0] = jnp.where(left, first, second).astype(BF16)
                    done[half, 2 * pair + i, o, 1] = jnp.where(left, second, first).astype(BF16)


def along_y_kernel(place_ref, own_ref, other_ref, own_later, other_later, *rest):
    outs, turned, done = rest[:5], rest[5], rest[6]
    y, core = place_ref[1], place_ref[2]
    unit = (
        lax.broadcasted_iota(jnp.int32, (128, 128), 0) == lax.broadcasted_iota(jnp.int32, (128, 128), 1)
    ).astype(F32).astype(BF16)
    for o in range(OCC):
        for half in range(2):
            for i, ref in enumerate((own_ref, other_ref) if o < 4 else (own_later, other_later)):
                across = lax.dot_general(
                    unit, ref[o % 4, :, half * 128 : half * 128 + 128], (((1,), (1,)), ((), ())), preferred_element_type=F32
                )
                turned[half, pl.ds(o * 128, 128), pl.ds(i * ROWS, ROWS)] = across.astype(BF16)
    product(core, turned, own_ref, other_ref, done)
    for d in range(4):
        for h in range(2):
            which, at = PLACES[d, h]
            for u in range(2):
                for j in range(4):
                    for half in range(2):
                        part = done[half, j, h * 4 + lax.rem(y + d, 4), u]
                        if at is None:
                            outs[which][u, j, half] = part
                        else:
                            outs[which][at, u, j, half] = part


def along_x_kernel(place_ref, own_ref, other_ref, turned, *rest):
    outs, done = rest[:5], rest[5]
    x, core = place_ref[0], place_ref[2]
    product(core, turned, own_ref, other_ref, done)
    for d in range(4):
        to = lax.rem(x + d, 4)
        for h in range(2):
            which, at = PLACES[d, h]
            for u in range(2):
                for j in range(4):
                    for half in range(2):
                        part = done[half, j, to // 2 * 4 + h * 2 + u, lax.rem(to, 2)]
                        if at is None:
                            outs[which][u, j, half] = part
                        else:
                            outs[which][at, u, j, half] = part


PART = (4, 2, 64, 128)


def partial(place, own, other, own_later, other_later):
    pair = jax.ShapeDtypeStruct((2, 2) + PART, BF16)
    single = jax.ShapeDtypeStruct((2,) + PART, BF16)
    outs = [pair, pair, single, single, pair]
    done = pltpu.VMEM((2, 4, OCC, 2, 64, 128), BF16)
    *first, turned = pl.pallas_call(
        along_y_kernel,
        out_shape=outs + [jax.ShapeDtypeStruct((2, OCC * 128, 2 * ROWS), BF16)],
        in_specs=[SMEM] + [VMEM] * 4,
        out_specs=[VMEM] * 6,
        scratch_shapes=[done],
        compiler_params=params(10),
    )(place, own, other, own_later, other_later)
    second = pl.pallas_call(
        along_x_kernel,
        out_shape=outs,
        in_specs=[SMEM, VMEM, VMEM, VMEM],
        out_specs=[VMEM] * 5,
        scratch_shapes=[done],
        compiler_params=params(10),
    )(place, own_later, other_later, turned)
    return first, second


def first_sum_kernel(place_ref, own, from_back, from_ahead, last_back, last_ahead, *outs, at):
    for d in range(4):
        to = lax.rem(place_ref[at] + d, 4)
        h, u = to // 2, lax.rem(to, 2)
        for side, (one, two) in enumerate(((from_ahead, last_back), (from_back, last_ahead))):

            @pl.when(h == side)
            def _():
                total = own[side, u].astype(F32) + one[1, u].astype(F32) + two[u].astype(F32)
                outs[d][...] = total.astype(BF16)


def first_sum(place, at, ins):
    def kernel(*refs):
        first_sum_kernel(*refs, at=at)

    return pl.pallas_call(
        kernel,
        out_shape=[jax.ShapeDtypeStruct(PART, BF16)] * 4,
        in_specs=[SMEM] + [VMEM] * 5,
        out_specs=[VMEM] * 4,
        compiler_params=params(6),
    )(place, *ins)


def largest(x):
    return jnp.max(jnp.abs(x), axis=(0, 1), keepdims=True)


def power_above(x):
    return jnp.ceil(jnp.log2(jnp.maximum(x, TINY)))


def second_sum_kernel(*refs):
    ins, out = refs[:8], refs[8]
    for half in range(2):
        for j in range(4):
            total = ins[half * 4][j].astype(F32)
            for d in range(1, 4):
                total = total + ins[half * 4 + d][j].astype(F32)
            total = total.reshape(128, 128)
            power = power_above(largest(total))
            steps = jnp.round(total * jnp.exp2(-power) * STEPS)
            out[half * 4 + j, 0:128] = steps.astype(jnp.int32).astype(jnp.int16)
            out[half * 4 + j, 128:144] = jnp.broadcast_to(power, (16, 128)).astype(jnp.int32).astype(jnp.int16)


def second_sum(ins):
    return pl.pallas_call(
        second_sum_kernel,
        out_shape=jax.ShapeDtypeStruct((OCC, 144, 128), jnp.int16),
        in_specs=[VMEM] * 8,
        out_specs=VMEM,
        compiler_params=params(6),
    )(*ins)


def finish_kernel(place_ref, parts_ref, below_ref, out_ref):
    core, low = place_ref[2], place_ref[3]
    total = jnp.zeros((128, 128), F32)
    for z in range(8):
        power = parts_ref[z, 128:144].astype(jnp.int32).astype(F32)[0:1]
        total = total + parts_ref[z, 0:128].astype(jnp.int32).astype(F32) * (jnp.exp2(power) * (1.0 / STEPS))
    total = total.reshape(2, 64, 128)
    across = [total[half].T for half in range(2)]
    crossed = []
    for half in range(2):
        source = jnp.where(core == 0, across[half], across[1 - half])
        same = jnp.concatenate([source[0:64], source[64:128]], axis=1)
        other = jnp.concatenate([source[64:128], source[0:64]], axis=1)
        crossed.append(jnp.where(low == 0, same, other))
    amplitudes = [total[half] / below_ref[half] for half in range(2)]
    terms = [amplitudes[half] * (2.0 * total[half] - crossed[half]) for half in range(2)]
    energy = jnp.sum(terms[0] + terms[1], axis=(0, 1), keepdims=True)
    power = power_above(jnp.maximum(largest(amplitudes[0]), largest(amplitudes[1])))
    power_energy = power_above(jnp.abs(energy))
    scaled = energy * jnp.exp2(-power_energy) * STEPS
    high = jnp.round(scaled)
    lane = lax.broadcasted_iota(jnp.int32, (64, 128), 1)
    which = lax.rem(lane, 4)
    rest = jnp.where(which == 2, high, jnp.round((scaled - high) * STEPS))
    rest = jnp.where(which == 0, power, jnp.where(which == 1, power_energy, rest))
    quarter = lax.rem(lane // 64 + low, 2)
    for half in range(2):
        coded = jnp.round(amplitudes[half] * jnp.exp2(-power) * STEPS)
        for q in range(2):
            sent = jnp.where(quarter == q, coded, rest).astype(jnp.int32).reshape(8, 8, 128)
            out_ref[pl.ds(half * 16 + q * 8, 8)] = sent.astype(jnp.int16)


def finish(place, parts, below):
    return pl.pallas_call(
        finish_kernel,
        out_shape=jax.ShapeDtypeStruct((32, 8, 128), jnp.int16),
        in_specs=[SMEM, VMEM, VMEM],
        out_specs=VMEM,
        compiler_params=params(6),
    )(place, parts, below)


def collect_kernel(place_ref, parts_ref, amp_ref, pair_ref):
    block = place_ref[4]
    half, quarter = block // 16, lax.rem(block // 8, 2)
    lane = lax.broadcasted_iota(jnp.int32, (8, 128), 1)
    ours = lane // 64 == quarter
    coded, rests = [], []
    for j in range(OCC):
        for side in range(2):
            core = lax.rem(half + side, 2)
            one, two = (parts_ref[j * 4 + low * 2 + core].astype(jnp.int32).astype(F32) for low in range(2))
            coded.append(jnp.where(ours, one, two))
            rests.append(jnp.where(ours, two, one)[0:1])
    rest = jnp.concatenate(rests, axis=0)
    first = lax.broadcasted_iota(jnp.int32, (2 * OCC, 128), 1) < 64
    scale = jnp.where(first, jnp.exp2(rest[:, 64:65]), jnp.exp2(rest[:, 0:1])) * (1.0 / STEPS)
    shares = jnp.zeros((2 * OCC, 1), F32)
    for at in (0, 64):
        number = (rest[:, at + 2 : at + 3] + rest[:, at + 3 : at + 4] * (1.0 / STEPS)) * (1.0 / STEPS)
        shares = shares + number * jnp.exp2(rest[:, at + 1 : at + 2])
    energies = jnp.zeros((8, 128), F32)
    for j in range(OCC):
        for side in range(2):
            k = 2 * j + side
            amp = coded[k] * scale[k : k + 1]
            for r in range(8):
                amp_ref[r, pl.ds(j, 1), pl.ds(side * 128, 128)] = amp[r : r + 1, :]
        total = shares[2 * j : 2 * j + 1] + shares[2 * j + 1 : 2 * j + 2]
        energies = jnp.where(lane == j, jnp.broadcast_to(total, (8, 128)), energies)
    pair_ref[...] = energies[0:1, 0:OCC]


def collect(place, parts):
    return pl.pallas_call(
        collect_kernel,
        out_shape=[jax.ShapeDtypeStruct((8, OCC, VIR), F32), jax.ShapeDtypeStruct((1, OCC), F32)],
        in_specs=[SMEM, VMEM],
        out_specs=[VMEM, VMEM],
        compiler_params=params(6),
    )(place, parts)


def moved(x, axis, by):
    n = lax.axis_size(axis)
    return lax.ppermute(x, axis, [(i, (i + by) % n) for i in range(n)])


def denominators(eps_occ, eps_vir, occ_index, core, low):
    levels = jnp.take(eps_occ, occ_index)
    own = jnp.sum(jnp.where(jnp.arange(OCC) == lax.axis_index(AUX), levels, 0.0))
    other = jnp.sum(jnp.where(jnp.arange(OCC) == lax.axis_index("z"), levels, 0.0))
    quarters = eps_vir.reshape(2, 2, 64, 1)
    of_rows = jnp.where((jnp.arange(128) // 64 + low) % 2 == 0, quarters[:, 0], quarters[:, 1])
    halves = eps_vir.reshape(2, 1, 128)
    of_columns = jnp.where(core == 0, halves, halves[::-1])
    return own + other - of_rows - of_columns


def body(three_center, slot_block, slot_aux, live_slots, vir_coef, eps_occ, eps_vir, occ_index):
    x, y, core, low = lax.axis_index(X), lax.axis_index("y"), lax.axis_index("core"), lax.axis_index("xl")
    place = jnp.stack([x, y, core, low, lax.axis_index(BLK)]).astype(jnp.int32)
    own, weights, later = half_transform(slot_block, slot_aux, live_slots, three_center, vir_coef)
    other = moved(own, "core", 1)
    own_later = other_half(later, weights)
    other_later = moved(own_later, "core", 1)
    below = denominators(eps_occ, eps_vir, occ_index, core, low)
    other_later, below = lax.optimization_barrier((other_later, below))

    got = []
    for axis, (ahead, back, one, minus, mine) in zip(("y", X), partial(place, own, other, own_later, other_later)):
        got.append((axis, moved(ahead, axis, 1), moved(back, axis, -1), one, minus, mine))
    ins = []
    for at, (axis, from_back, from_ahead, one, minus, mine) in enumerate(got):
        one = (one.astype(F32) + from_back[0].astype(F32)).astype(BF16)
        minus = (minus.astype(F32) + from_ahead[0].astype(F32)).astype(BF16)
        last = moved(one, axis, 1), moved(minus, axis, -1)
        group = first_sum(place, at, (mine, from_back, from_ahead, *last))
        ins += [group[0]] + [moved(group[d], (X, "y")[at], d) for d in (2, 1, 3)]
    parts = lax.all_to_all(second_sum(ins), "z", 0, 0, tiled=True)
    sent = finish(place, parts, below)
    amplitudes, pair = collect(place, lax.all_to_all(sent, BLK, 0, 0, tiled=True))
    return amplitudes[None], pair


def solution(mesh):
    fine = Mesh(mesh.devices.reshape(2, 4, 8, 2, 2), ("xh", "y", "z", "xl", "core"))
    every = AUX + BLK
    in_specs = (P(every, None, None, None), P(every), P(every), P(every), P(), P(), P(), P())
    out_specs = (P(AUX, BLK, None, None), P(AUX, None))
    return jax.shard_map(body, mesh=fine, in_specs=in_specs, out_specs=out_specs, check_vma=False)
```
